128 devices in a mesh: tm: 4 (over z_lo, core), stn: 32 (over z_hi, y, x).
Axes of the slice: x: 4, y: 4, z: 4 (z_hi: 2, z_lo: 2; z = z_hi * 2 + z_lo), core: 2. Of those that a mesh axis runs over, the one named last changes fastest.
Arguments:
- baseband: bfloat16 [128, 2, 2, 524288], P('stn', None, None, 'tm'), may hold values from -6 to 6
- delays: int32 [128], P('stn'), may hold values from 0 to 4096, as said below
- fir_coeffs: float32 [16, 1024], replicated, may hold values from -1.5 to 1.5
- beam_weights: bfloat16 [1024, 2, 128, 1024], P('stn'), may hold values from -0.375 to 0.375
Outputs:
- beam_power: bfloat16 [1024, 512, 1024], P('stn', 'tm')
The draws below stay inside these ranges and needn't reach their ends.
Inputs may be any that keep to these rules, and one draw needn't show every extreme that they name: `delays`: some station's delay equals 4096 in every draw.
All inputs are finite; a program needn't handle non-finite values.
Results may differ from the reference program's by a relative error of at most 0.0056.
Values may be sent and summed in bfloat16 or wider, within the bound.
A program may use at most 256 MiB of HBM per device.

```python
import math
import jax
import jax.numpy as jnp
from jax import lax

CH = 1024
TAPS = 16
BEAMS = 1024
DMAX = 4096
STATIONS = 128
NSPEC = 512
SAMPLES = 524288


def draw_delays(key, part):
    key = jax.random.fold_in(key, 11)
    first, second = jax.random.split(key)
    uniform_draw = jax.random.randint(first, (STATIONS,), 0, DMAX + 1, dtype=jnp.int32)
    chosen = jax.random.randint(second, (), 0, STATIONS, dtype=jnp.int32)
    return jnp.where(jnp.arange(STATIONS, dtype=jnp.int32) == chosen, DMAX, uniform_draw)


def shard_levels(key, dims, cuts, smallest, high):
    loudness, own = 1.0, jax.random.fold_in(key, 6)
    for axis_at, shards_of in cuts:
        steps = jnp.exp(jax.random.uniform(jax.random.fold_in(own, axis_at), (shards_of,), jnp.float32, smallest / len(cuts), high / len(cuts)))
        loudness = loudness * jnp.repeat(steps, dims[axis_at] // shards_of).reshape([-1 if axis == axis_at else 1 for axis in range(len(dims))])
    return loudness


def centred(key, extent, spread, most, pieces=(), kind=jnp.bfloat16):
    drawn = jax.random.normal(key, extent, jnp.float32) * spread
    if len(pieces) > 0:
        drawn = shard_levels(key, extent, pieces, -0.22, 0.18) * drawn
    return jnp.clip(drawn, min=-most, max=most).astype(kind)


def setup_inputs(seed: int = 0) -> dict:
    keys = jax.random.split(jax.random.key(seed), 5)
    baseband = centred(keys[0], (STATIONS, 2, 2, SAMPLES), 1.0, 6.0, ((0, 32), (3, 4)))
    delays = draw_delays(jax.random.fold_in(keys[4], 71), 0)
    fir_coeffs = centred(keys[2], (TAPS, CH), TAPS ** -0.5, 1.5, (), jnp.float32)
    beam_weights = centred(keys[3], (CH, 2, STATIONS, BEAMS), (2 * STATIONS) ** -0.5, 0.375, ((0, 32),))
    return dict(baseband=baseband, delays=delays, fir_coeffs=fir_coeffs, beam_weights=beam_weights)


def dft_table(length):
    indices = jnp.arange(length, dtype=jnp.int32)
    phases = indices[:, None] * indices[None, :] % length
    angles = phases.astype(jnp.float32) * (2.0 * math.pi / length)
    cosine = jnp.cos(angles) / math.sqrt(length)
    sines = jnp.sin(angles) / math.sqrt(length)
    upper_rows = jnp.concatenate([cosine, sines], 1)
    bottom = jnp.concatenate([-sines, cosine], 1)
    return jnp.concatenate([upper_rows, bottom], 0).astype(jnp.bfloat16)

def reference(baseband, delays, fir_coeffs, beam_weights):
    lead_samples = (TAPS - 1) * CH
    padded = jnp.pad(baseband, ((0, 0), (0, 0), (0, 0), (lead_samples, DMAX)))

    def delay_window(station_row, offset):
        return lax.dynamic_slice_in_dim(station_row, offset.astype(jnp.int32), lead_samples + SAMPLES, 2)
    delayed = jax.vmap(delay_window)(padded, delays)
    frames = delayed.reshape(STATIONS, 2, 2, NSPEC + TAPS - 1, CH)
    twiddles = dft_table(CH)

    def channelize(station_frames):
        filter_sum = jnp.zeros((2, 2, NSPEC, CH), jnp.float32)
        for tap_index in range(TAPS):
            filter_sum = filter_sum + fir_coeffs[tap_index] * station_frames[:, :, tap_index:tap_index + NSPEC, :].astype(jnp.float32)
        filtered = filter_sum.astype(jnp.bfloat16)
        rows = jnp.transpose(filtered, (0, 2, 1, 3)).reshape(2 * NSPEC, 2 * CH)
        return jnp.dot(rows, twiddles.T, preferred_element_type=jnp.float32).astype(jnp.bfloat16)
    spectra = lax.map(channelize, frames)
    voltages = spectra.reshape(STATIONS, 2, NSPEC, 2, CH)
    chan_block = 8

    def beam_block(first_chan):
        piece_volts = lax.dynamic_slice_in_dim(voltages, first_chan, chan_block, 4).astype(jnp.float32)
        weights = lax.dynamic_slice_in_dim(beam_weights, first_chan, chan_block, 0).astype(jnp.float32)
        pattern = 'spmc,csb->cpmb'
        real_part = jnp.einsum(pattern, piece_volts[:, :, :, 0], weights[:, 0]) - jnp.einsum(pattern, piece_volts[:, :, :, 1], weights[:, 1])
        imag_part = jnp.einsum(pattern, piece_volts[:, :, :, 0], weights[:, 1]) + jnp.einsum(pattern, piece_volts[:, :, :, 1], weights[:, 0])
        return lax.optimization_barrier(jnp.sum(real_part * real_part + imag_part * imag_part, axis=1)).astype(jnp.bfloat16)
    starts = jnp.arange(CH // chan_block, dtype=jnp.int32) * chan_block
    return lax.map(beam_block, starts).reshape(CH, NSPEC, BEAMS)
```

```python
import math

import jax
import jax.numpy as jnp
import ml_dtypes
import numpy as np
from jax import lax
from jax.experimental import pallas as pl
from jax.experimental.pallas import tpu as pltpu
from jax.sharding import PartitionSpec as P

MESH = pl.DeviceIdType.MESH
BF, F32 = jnp.bfloat16, jnp.float32
CH, TAPS, BEAMS, DMAX = 1024, 16, 1024, 4096
PEERS = 32
LOCAL = 4
PER = CH // PEERS
MLOC = 128
HALF = MLOC // 2
FIRST = 16
LEAD = TAPS - 1
FRAMES = LEAD + MLOC + DMAX // CH
ROWS = FRAMES * 16 + 16
LEAD_ROWS, OWN_ROWS, TRAIL_ROWS = LEAD * 16, MLOC * 16, DMAX // CH * 16
FS = 136
XS = 136


def twiddle_table():
    n = np.arange(CH // 4)
    out = np.zeros((4, PEERS, PER // 4, 2, 2, CH // 4), np.float64)
    for r in range(4):
        k = PER * np.arange(PEERS)[:, None] + 4 * np.arange(PER // 4)[None, :] + r
        angle = 2 * np.pi * ((k[:, :, None] * n) % CH) / CH
        cosine, sine = np.cos(angle) / math.sqrt(CH), np.sin(angle) / math.sqrt(CH)
        out[r, :, :, 0, 0], out[r, :, :, 0, 1] = cosine, sine
        out[r, :, :, 1, 0], out[r, :, :, 1, 1] = -sine, cosine
    return out.reshape(4, CH // 2, CH // 2).astype(ml_dtypes.bfloat16)


def kernel(delays, coef, base, weights, table, out, raw, E, C, Fq, F, T, S, R, W, X, O,
           base_sem, table_sem, weight_sem, halo_send, halo_recv, send_sem, recv_sem, out_sem):
    t, me = lax.axis_index("tm"), lax.axis_index("stn")
    mz, my, mx = me // 16, (me // 4) % 4, me % 4

    def peer(i):
        q = (i * 13) % PEERS
        return ((mz + q // 16) % 2) * 16 + ((my + (q // 4) % 4) % 4) * 4 + (mx + q % 4) % 4

    def at(stn):
        return {"tm": t, "stn": stn}

    barrier = pltpu.get_barrier_semaphore()

    def greet(i, carry):
        pl.semaphore_signal(barrier, inc=1, device_id=at(peer(i)), device_id_type=MESH)
        return carry

    lax.fori_loop(1, PEERS, greet, 0)

    @pl.when(t > 0)
    def _():
        pl.semaphore_signal(barrier, inc=1, device_id={"tm": t - 1, "stn": me}, device_id_type=MESH)

    @pl.when(t < 3)
    def _():
        pl.semaphore_signal(barrier, inc=1, device_id={"tm": t + 1, "stn": me}, device_id_type=MESH)

    def base_copy(s):
        return pltpu.make_async_copy(base.at[s], raw.at[s, :, pl.ds(LEAD_ROWS, OWN_ROWS)], base_sem.at[s])

    for s in range(LOCAL):
        base_copy(s).start()
    table_copy = pltpu.make_async_copy(table, T, table_sem)
    table_copy.start()
    weight_copy = pltpu.make_async_copy(weights, W, weight_sem)

    for k in range(TAPS):
        for j in range(8):
            pair = jnp.broadcast_to(coef[k : k + 1, 128 * j : 128 * j + 128], (2, 128))
            C[k, j // 4, 2 * (j % 4) : 2 * (j % 4) + 2, :] = pair
    raw[:, :, FRAMES * 16 :, :] = jnp.zeros((LOCAL, 2, 16, 128), BF)

    @pl.when(t == 0)
    def _():
        raw[:, :, :LEAD_ROWS, :] = jnp.zeros((LOCAL, 2, LEAD_ROWS, 128), BF)

    @pl.when(t == 3)
    def _():
        raw[:, :, LEAD_ROWS + OWN_ROWS : FRAMES * 16, :] = jnp.zeros((LOCAL, 2, TRAIL_ROWS, 128), BF)

    to_next = pltpu.make_async_remote_copy(
        base.at[:, :, pl.ds(OWN_ROWS - LEAD_ROWS, LEAD_ROWS)], raw.at[:, :, pl.ds(0, LEAD_ROWS)],
        halo_send.at[0], halo_recv.at[0], device_id={"tm": t + 1, "stn": me}, device_id_type=MESH)
    to_last = pltpu.make_async_remote_copy(
        base.at[:, :, pl.ds(0, TRAIL_ROWS)], raw.at[:, :, pl.ds(LEAD_ROWS + OWN_ROWS, TRAIL_ROWS)],
        halo_send.at[1], halo_recv.at[1], device_id={"tm": t - 1, "stn": me}, device_id_type=MESH)

    def rotate(s, shift, first, count):
        j = lax.broadcasted_iota(jnp.int32, (128, 128), 0)
        lane = lax.broadcasted_iota(jnp.int32, (128, 128), 1)
        rotation = jnp.where((j == lane + shift) | (j == lane + shift - 128), 1.0, 0.0).astype(BF)

        def body(p, carry):
            rows = pl.ds(first * 16, count * 16)
            E[s, p, rows, :] = jnp.dot(raw[s, p, rows, :], rotation, preferred_element_type=F32)
            return carry

        lax.fori_loop(0, 2, body, 0)

    def fir(s, h, tiles, shift):
        keep = lax.broadcasted_iota(jnp.int32, (8, 128), 1) < 128 - shift

        def body(it, carry):
            i, p, half = it // 4, (it // 2) % 2, it % 2
            first = (FIRST + HALF * h + 16 * i) % MLOC
            d = []
            for f in range(31):
                row = (first + f) * 16 + half * 8 + 2 * tiles
                d.append(jnp.where(keep, E[s, p, pl.ds(row, 8), :], E[s, p, pl.ds(row + 2, 8), :]))
            for m in range(16):
                total = C[0, half] * d[m]
                for k in range(1, TAPS):
                    total = total + C[k, half] * d[m + k]
                Fq[pl.ds(half * 8 * FS + p * HALF + i * 16 + m, 8, stride=FS), :] = total
            return carry

        lax.fori_loop(0, 16, body, 0)

    def butterfly(place):
        def body(block, carry):
            rows = pl.multiple_of(block * 16, 16)
            for low in range(2):
                x = [[Fq[pl.ds(rows + ((2 * q + low) * 2 + c) * FS, 16), :] for q in range(4)] for c in range(2)]
                t0, t1 = [v[0] + v[2] for v in x], [v[0] - v[2] for v in x]
                t2, t3 = [v[1] + v[3] for v in x], [v[1] - v[3] for v in x]
                y = [
                    [t0[0] + t2[0], t0[1] + t2[1]],
                    [t1[0] + t3[1], t1[1] - t3[0]],
                    [t0[0] - t2[0], t0[1] - t2[1]],
                    [t1[0] - t3[1], t1[1] + t3[0]],
                ]
                for r in range(4):
                    for c in range(2):
                        lanes = c * 256 + low * 128
                        F[r, pl.ds(place * 128 + rows, 16), lanes : lanes + 128] = y[r][c].astype(BF)
            return carry

        lax.fori_loop(0, 8, body, 0)

    def transform(h, pair):
        def body(r, carry):
            spectra = lax.dot_general(T[r], F[r], (((1,), (1,)), ((), ())), preferred_element_type=F32).astype(BF)
            for i in range(2):
                S[h, r, :, 2 * pair + i] = spectra[:, 128 * i : 128 * i + 128].reshape(PEERS, 16, 128)
            return carry

        lax.fori_loop(0, 4, body, 0)

    def unit(h, pair):
        def body(i, carry):
            s = 2 * pair + i
            delay = delays[s]
            tiles, shift = delay // 128, delay % 128
            if h == 0:
                base_copy(s).wait()
                rotate(s, shift, 16, 84)
            else:
                rotate(s, shift, 0, 16)
                rotate(s, shift, 100, 48)
            fir(s, h, tiles, shift)
            butterfly(i)
            return carry

        lax.fori_loop(0, 2, body, 0)
        if h == 0:
            pl.when(pair == 0)(table_copy.wait)
        transform(h, pair)

    def send_first(pair):
        def body(i, carry):
            d = peer(i)
            both = pl.ds(2 * pair, 2)
            pltpu.make_async_remote_copy(
                S.at[0, :, d, both], R.at[0, :, me, both], send_sem.at[0], recv_sem.at[0],
                device_id=at(d), device_id_type=MESH).start()
            return carry

        lax.fori_loop(1, PEERS, body, 0)

    def send_second(r):
        def body(i, carry):
            d = peer(i)
            pltpu.make_async_remote_copy(
                S.at[1, r, d], R.at[1, r, me], send_sem.at[1 + r], recv_sem.at[1 + r],
                device_id=at(d), device_id_type=MESH).start()
            return carry

        lax.fori_loop(1, PEERS, body, 0)
        pltpu.make_async_copy(S.at[1, r, me], R.at[1, r, me], recv_sem.at[1 + r]).start()

    def interleave(h, r):
        def body(g, carry):
            for s in range(LOCAL):
                X[pl.ds(g * LOCAL + s, 16, stride=XS), :] = R[h, r, g, s].astype(F32)
            return carry

        lax.fori_loop(0, PEERS, body, 0, unroll=2)

    def beams(h, r):
        def body(j, carry):
            rows = [pl.ds(pl.multiple_of((2 * j + c) * XS, 8), 128) for c in range(2)]
            re, im = [X[v, :].astype(BF).T for v in rows]
            lhs = jnp.concatenate([jnp.concatenate([re, -im], 1), jnp.concatenate([im, re], 1)], 0)
            y = jnp.dot(lhs, W[j, r], preferred_element_type=F32)
            y = y * y
            power = (y[:HALF] + y[HALF : 2 * HALF]) + (y[2 * HALF : 3 * HALF] + y[3 * HALF :])
            O[h, r, j] = power.astype(BF)
            return carry

        lax.fori_loop(0, PER // 4, body, 0)

    unit(0, 0)
    pl.semaphore_wait(barrier, PEERS - 1 + (t + 2) // 3 + (5 - t) // 3)
    pl.when(t > 0)(to_last.start)
    pl.when(t < 3)(to_next.start)

    send_first(0)
    weight_copy.start()
    unit(0, 1)
    send_first(1)
    pltpu.make_async_copy(S.at[0, :, me], R.at[0, :, me], recv_sem.at[0]).start()

    @pl.when(t > 0)
    def _():
        to_next.wait_recv()

    @pl.when(t < 3)
    def _():
        to_last.wait_recv()

    def second(pair, carry):
        unit(1, pair)
        return carry

    lax.fori_loop(0, 2, second, 0)

    def second_sends(r, carry):
        send_second(r)
        return carry

    lax.fori_loop(0, 4, second_sends, 0)

    weight_copy.wait()
    pltpu.make_async_copy(R.at[0], R.at[0], recv_sem.at[0]).wait()

    def finish_first(r, carry):
        interleave(0, r)
        beams(0, r)
        pltpu.make_async_copy(O.at[0, r], out.at[:, r, pl.ds(FIRST, HALF)], out_sem).start()
        return carry

    lax.fori_loop(0, 4, finish_first, 0)

    def finish_second(r, carry):
        pltpu.make_async_copy(R.at[1, r], R.at[1, r], recv_sem.at[1 + r]).wait()
        interleave(1, r)
        beams(1, r)
        head = MLOC - FIRST - HALF
        pltpu.make_async_copy(O.at[1, r, :, pl.ds(0, head)], out.at[:, r, pl.ds(FIRST + HALF, head)], out_sem).start()
        pltpu.make_async_copy(O.at[1, r, :, pl.ds(head, FIRST)], out.at[:, r, pl.ds(0, FIRST)], out_sem).start()
        return carry

    lax.fori_loop(0, 4, finish_second, 0)

    sent = pl.ds(0, PEERS - 1)
    pltpu.make_async_copy(S.at[0, :, sent], S.at[0, :, sent], send_sem.at[0]).wait()

    def sent_second(r, carry):
        pltpu.make_async_copy(S.at[1, r, sent], S.at[1, r, sent], send_sem.at[1 + r]).wait()
        return carry

    lax.fori_loop(0, 4, sent_second, 0)

    @pl.when(t > 0)
    def _():
        to_last.wait_send()

    @pl.when(t < 3)
    def _():
        to_next.wait_send()

    pltpu.make_async_copy(out, out, out_sem).wait()


def per_device(baseband, delays, fir_coeffs, beam_weights):
    rows = baseband.reshape(LOCAL, 2, 2, OWN_ROWS // 2, 128).transpose(0, 1, 3, 2, 4).reshape(LOCAL, 2, OWN_ROWS, 128)
    weights = beam_weights.reshape(PER // 4, 4, 2 * LOCAL * PEERS, BEAMS)
    anywhere = pl.BlockSpec(memory_space=pl.ANY)
    power = pl.pallas_call(
        kernel,
        out_shape=jax.ShapeDtypeStruct((PER // 4, 4, MLOC, BEAMS), BF),
        in_specs=[pl.BlockSpec(memory_space=pltpu.SMEM), pl.BlockSpec(memory_space=pltpu.VMEM), anywhere, anywhere, anywhere],
        out_specs=anywhere,
        scratch_shapes=[
            pltpu.VMEM((LOCAL, 2, ROWS, 128), BF),
            pltpu.VMEM((LOCAL, 2, ROWS, 128), F32),
            pltpu.VMEM((TAPS, 2, 8, 128), F32),
            pltpu.VMEM((16 * FS, 128), F32),
            pltpu.VMEM((4, 256, CH // 2), BF),
            pltpu.VMEM((4, CH // 2, CH // 2), BF),
            pltpu.VMEM((2, 4, PEERS, LOCAL, 16, 128), BF),
            pltpu.VMEM((2, 4, PEERS, LOCAL, 16, 128), BF),
            pltpu.VMEM((PER // 4, 4, 2 * LOCAL * PEERS, BEAMS), BF),
            pltpu.VMEM((16 * XS, 128), F32),
            pltpu.VMEM((2, 4, PER // 4, HALF, BEAMS), BF),
            pltpu.SemaphoreType.DMA((LOCAL,)),
            pltpu.SemaphoreType.DMA,
            pltpu.SemaphoreType.DMA,
            pltpu.SemaphoreType.DMA((2,)),
            pltpu.SemaphoreType.DMA((2,)),
            pltpu.SemaphoreType.DMA((5,)),
            pltpu.SemaphoreType.DMA((5,)),
            pltpu.SemaphoreType.DMA,
        ],
        compiler_params=pltpu.CompilerParams(collective_id=0, has_side_effects=True, vmem_limit_bytes=60 << 20),
        name="channelize_beams",
    )(delays, fir_coeffs, rows, weights, jnp.asarray(twiddle_table()))
    return power.reshape(PER, MLOC, BEAMS)


def solution(mesh):
    placed = (P("stn", None, None, "tm"), P("stn"), P(), P("stn", None, None, None))
    return jax.shard_map(
        per_device, mesh=mesh, in_specs=placed, out_specs=P("stn", "tm", None), check_vma=False
    )
```

```python
import math

import jax
import jax.numpy as jnp
import ml_dtypes
import numpy as np
from jax import lax
from jax.experimental import pallas as pl
from jax.experimental.pallas import tpu as pltpu
from jax.sharding import PartitionSpec as P

MESH = pl.DeviceIdType.MESH
BF, F32 = jnp.bfloat16, jnp.float32
CH, TAPS, BEAMS, DMAX = 1024, 16, 1024, 4096
PEERS = 32
LOCAL = 4
PER = CH // PEERS
MLOC = 128
HALF = MLOC // 2
FIRST = 16
LEAD = TAPS - 1
FRAMES = LEAD + MLOC + DMAX // CH
ROWS = FRAMES * 16 + 16
LEAD_ROWS, OWN_ROWS, TRAIL_ROWS = LEAD * 16, MLOC * 16, DMAX // CH * 16
FS = 136
XS = 136


def twiddle_table():
    n = np.arange(CH // 4)
    out = np.zeros((4, PEERS, PER // 4, 2, 2, CH // 4), np.float64)
    for r in range(4):
        k = PER * np.arange(PEERS)[:, None] + 4 * np.arange(PER // 4)[None, :] + r
        angle = 2 * np.pi * ((k[:, :, None] * n) % CH) / CH
        cosine, sine = np.cos(angle) / math.sqrt(CH), np.sin(angle) / math.sqrt(CH)
        out[r, :, :, 0, 0], out[r, :, :, 0, 1] = cosine, sine
        out[r, :, :, 1, 0], out[r, :, :, 1, 1] = -sine, cosine
    return out.reshape(4, CH // 2, CH // 2).astype(ml_dtypes.bfloat16)


def kernel(delays, coef, base, weights, table, out, raw, E, C, Fq, F, T, S, R, W, X,
           base_sem, table_sem, weight_sem, halo_send, halo_recv, send_sem, recv_sem):
    t, me = lax.axis_index("tm"), lax.axis_index("stn")
    mz, my, mx = me // 16, (me // 4) % 4, me % 4

    def peer(i):
        q = (i * 13) % PEERS
        return ((mz + q // 16) % 2) * 16 + ((my + (q // 4) % 4) % 4) * 4 + (mx + q % 4) % 4

    def at(stn):
        return {"tm": t, "stn": stn}

    barrier = pltpu.get_barrier_semaphore()

    def greet(i, carry):
        pl.semaphore_signal(barrier, inc=1, device_id=at(peer(i)), device_id_type=MESH)
        return carry

    lax.fori_loop(1, PEERS, greet, 0)

    @pl.when(t > 0)
    def _():
        pl.semaphore_signal(barrier, inc=1, device_id={"tm": t - 1, "stn": me}, device_id_type=MESH)

    @pl.when(t < 3)
    def _():
        pl.semaphore_signal(barrier, inc=1, device_id={"tm": t + 1, "stn": me}, device_id_type=MESH)

    def base_copy(s):
        return pltpu.make_async_copy(base.at[s], raw.at[s, :, pl.ds(LEAD_ROWS, OWN_ROWS)], base_sem.at[s])

    for s in range(LOCAL):
        base_copy(s).start()
    table_copy = pltpu.make_async_copy(table, T, table_sem)
    table_copy.start()
    weight_copy = pltpu.make_async_copy(weights, W, weight_sem)

    for k in range(TAPS):
        for j in range(8):
            pair = jnp.broadcast_to(coef[k : k + 1, 128 * j : 128 * j + 128], (2, 128))
            C[k, j // 4, 2 * (j % 4) : 2 * (j % 4) + 2, :] = pair
    raw[:, :, FRAMES * 16 :, :] = jnp.zeros((LOCAL, 2, 16, 128), BF)

    @pl.when(t == 0)
    def _():
        raw[:, :, :LEAD_ROWS, :] = jnp.zeros((LOCAL, 2, LEAD_ROWS, 128), BF)

    @pl.when(t == 3)
    def _():
        raw[:, :, LEAD_ROWS + OWN_ROWS : FRAMES * 16, :] = jnp.zeros((LOCAL, 2, TRAIL_ROWS, 128), BF)

    to_next = pltpu.make_async_remote_copy(
        base.at[:, :, pl.ds(OWN_ROWS - LEAD_ROWS, LEAD_ROWS)], raw.at[:, :, pl.ds(0, LEAD_ROWS)],
        halo_send.at[0], halo_recv.at[0], device_id={"tm": t + 1, "stn": me}, device_id_type=MESH)
    to_last = pltpu.make_async_remote_copy(
        base.at[:, :, pl.ds(0, TRAIL_ROWS)], raw.at[:, :, pl.ds(LEAD_ROWS + OWN_ROWS, TRAIL_ROWS)],
        halo_send.at[1], halo_recv.at[1], device_id={"tm": t - 1, "stn": me}, device_id_type=MESH)

    def rotate(s, shift, first, count):
        j = lax.broadcasted_iota(jnp.int32, (128, 128), 0)
        lane = lax.broadcasted_iota(jnp.int32, (128, 128), 1)
        rotation = jnp.where((j == lane + shift) | (j == lane + shift - 128), 1.0, 0.0).astype(BF)

        def body(p, carry):
            rows = pl.ds(first * 16, count * 16)
            E[s, p, rows, :] = jnp.dot(raw[s, p, rows, :], rotation, preferred_element_type=F32)
            return carry

        lax.fori_loop(0, 2, body, 0)

    def fir(s, h, tiles, shift):
        keep = lax.broadcasted_iota(jnp.int32, (8, 128), 1) < 128 - shift

        def body(it, carry):
            i, p, half = it // 4, (it // 2) % 2, it % 2
            first = (FIRST + HALF * h + 16 * i) % MLOC
            d = []
            for f in range(31):
                row = (first + f) * 16 + half * 8 + 2 * tiles
                d.append(jnp.where(keep, E[s, p, pl.ds(row, 8), :], E[s, p, pl.ds(row + 2, 8), :]))
            for m in range(16):
                total = C[0, half] * d[m]
                for k in range(1, TAPS):
                    total = total + C[k, half] * d[m + k]
                Fq[pl.ds(half * 8 * FS + p * HALF + i * 16 + m, 8, stride=FS), :] = total
            return carry

        lax.fori_loop(0, 16, body, 0)

    def butterfly(place):
        def body(block, carry):
            rows = pl.multiple_of(block * 16, 16)
            for low in range(2):
                x = [[Fq[pl.ds(rows + ((2 * q + low) * 2 + c) * FS, 16), :] for q in range(4)] for c in range(2)]
                t0, t1 = [v[0] + v[2] for v in x], [v[0] - v[2] for v in x]
                t2, t3 = [v[1] + v[3] for v in x], [v[1] - v[3] for v in x]
                y = [
                    [t0[0] + t2[0], t0[1] + t2[1]],
                    [t1[0] + t3[1], t1[1] - t3[0]],
                    [t0[0] - t2[0], t0[1] - t2[1]],
                    [t1[0] - t3[1], t1[1] + t3[0]],
                ]
                for r in range(4):
                    for c in range(2):
                        lanes = c * 256 + low * 128
                        F[r, pl.ds(place * 128 + rows, 16), lanes : lanes + 128] = y[r][c].astype(BF)
            return carry

        lax.fori_loop(0, 8, body, 0)

    def transform(h, pair):
        def body(r, carry):
            spectra = lax.dot_general(T[r], F[r], (((1,), (1,)), ((), ())), preferred_element_type=F32).astype(BF)
            for i in range(2):
                S[h, r, :, 2 * pair + i] = spectra[:, 128 * i : 128 * i + 128].reshape(PEERS, 16, 128)
            return carry

        lax.fori_loop(0, 4, body, 0)

    def unit(h, pair):
        def body(i, carry):
            s = 2 * pair + i
            delay = delays[s]
            tiles, shift = delay // 128, delay % 128
            if h == 0:
                @pl.when(pair == 1)
                def _():
                    base_copy(s).wait()
                    rotate(s, shift, 16, 84)
            else:
                rotate(s, shift, 0, 16)
                rotate(s, shift, 100, 48)
            fir(s, h, tiles, shift)
            butterfly(i)
            return carry

        lax.fori_loop(0, 2, body, 0)
        if h == 0:
            pl.when(pair == 0)(table_copy.wait)
        transform(h, pair)

    def send_first(pair):
        def body(i, carry):
            d = peer(i)
            both = pl.ds(2 * pair, 2)
            pltpu.make_async_remote_copy(
                S.at[0, :, d, both], R.at[0, :, me, both], send_sem.at[0], recv_sem.at[0],
                device_id=at(d), device_id_type=MESH).start()
            return carry

        lax.fori_loop(1, PEERS, body, 0)

    def send_second(r):
        def body(i, carry):
            d = peer(i)
            pltpu.make_async_remote_copy(
                S.at[1, r, d], R.at[1, r, me], send_sem.at[1 + r], recv_sem.at[1 + r],
                device_id=at(d), device_id_type=MESH).start()
            return carry

        lax.fori_loop(1, PEERS, body, 0)
        pltpu.make_async_copy(S.at[1, r, me], R.at[1, r, me], recv_sem.at[1 + r]).start()

    def interleave(h, r):
        def body(g, carry):
            for s in range(LOCAL):
                X[pl.ds(g * LOCAL + s, 16, stride=XS), :] = R[h, r, g, s].astype(F32)
            return carry

        lax.fori_loop(0, PEERS, body, 0, unroll=2)

    def beams(h, r):
        def body(j, carry):
            rows = [pl.ds(pl.multiple_of((2 * j + c) * XS, 8), 128) for c in range(2)]
            re, im = [X[v, :].astype(BF).T for v in rows]
            lhs = jnp.concatenate([jnp.concatenate([re, -im], 1), jnp.concatenate([im, re], 1)], 0)
            y = jnp.dot(lhs, W[j, r], preferred_element_type=F32)
            y = y * y
            power = (y[:HALF] + y[HALF : 2 * HALF]) + (y[2 * HALF : 3 * HALF] + y[3 * HALF :])
            power = power.astype(BF)
            if h == 0:
                out[j, r, FIRST : FIRST + HALF, :] = power
            else:
                out[j, r, FIRST + HALF :, :] = power[: MLOC - FIRST - HALF]
                out[j, r, :FIRST, :] = power[MLOC - FIRST - HALF :]
            return carry

        lax.fori_loop(0, PER // 4, body, 0)

    for s in range(2):
        base_copy(s).wait()
        rotate(s, delays[s] % 128, 16, 84)
    pl.semaphore_wait(barrier, PEERS - 1 + (t + 2) // 3 + (5 - t) // 3)
    pl.when(t > 0)(to_last.start)
    pl.when(t < 3)(to_next.start)
    unit(0, 0)

    send_first(0)
    weight_copy.start()
    unit(0, 1)
    send_first(1)
    pltpu.make_async_copy(S.at[0, :, me], R.at[0, :, me], recv_sem.at[0]).start()

    @pl.when(t > 0)
    def _():
        to_next.wait_recv()

    @pl.when(t < 3)
    def _():
        to_last.wait_recv()

    def second(pair, carry):
        unit(1, pair)
        return carry

    lax.fori_loop(0, 2, second, 0)

    def second_sends(r, carry):
        send_second(r)
        return carry

    lax.fori_loop(0, 4, second_sends, 0)

    weight_copy.wait()
    pltpu.make_async_copy(R.at[0], R.at[0], recv_sem.at[0]).wait()

    def finish_first(r, carry):
        interleave(0, r)
        beams(0, r)
        return carry

    lax.fori_loop(0, 4, finish_first, 0)

    def finish_second(r, carry):
        pltpu.make_async_copy(R.at[1, r], R.at[1, r], recv_sem.at[1 + r]).wait()
        interleave(1, r)
        beams(1, r)
        return carry

    lax.fori_loop(0, 4, finish_second, 0)
    sent = pl.ds(0, PEERS - 1)
    pltpu.make_async_copy(S.at[0, :, sent], S.at[0, :, sent], send_sem.at[0]).wait()

    def sent_second(r, carry):
        pltpu.make_async_copy(S.at[1, r, sent], S.at[1, r, sent], send_sem.at[1 + r]).wait()
        return carry

    lax.fori_loop(0, 4, sent_second, 0)

    @pl.when(t > 0)
    def _():
        to_last.wait_send()

    @pl.when(t < 3)
    def _():
        to_next.wait_send()


def per_device(baseband, delays, fir_coeffs, beam_weights):
    rows = baseband.reshape(LOCAL, 2, 2, OWN_ROWS // 2, 128).transpose(0, 1, 3, 2, 4).reshape(LOCAL, 2, OWN_ROWS, 128)
    weights = beam_weights.reshape(PER // 4, 4, 2 * LOCAL * PEERS, BEAMS)
    anywhere = pl.BlockSpec(memory_space=pl.ANY)
    power = pl.pallas_call(
        kernel,
        out_shape=pltpu.VMEM((PER // 4, 4, MLOC, BEAMS), BF),
        in_specs=[pl.BlockSpec(memory_space=pltpu.SMEM), pl.BlockSpec(memory_space=pltpu.VMEM), anywhere, anywhere, anywhere],
        out_specs=pl.BlockSpec(memory_space=pltpu.VMEM),
        scratch_shapes=[
            pltpu.VMEM((LOCAL, 2, ROWS, 128), BF),
            pltpu.VMEM((LOCAL, 2, ROWS, 128), F32),
            pltpu.VMEM((TAPS, 2, 8, 128), F32),
            pltpu.VMEM((16 * FS, 128), F32),
            pltpu.VMEM((4, 256, CH // 2), BF),
            pltpu.VMEM((4, CH // 2, CH // 2), BF),
            pltpu.VMEM((2, 4, PEERS, LOCAL, 16, 128), BF),
            pltpu.VMEM((2, 4, PEERS, LOCAL, 16, 128), BF),
            pltpu.VMEM((PER // 4, 4, 2 * LOCAL * PEERS, BEAMS), BF),
            pltpu.VMEM((16 * XS, 128), F32),
            pltpu.SemaphoreType.DMA((LOCAL,)),
            pltpu.SemaphoreType.DMA,
            pltpu.SemaphoreType.DMA,
            pltpu.SemaphoreType.DMA((2,)),
            pltpu.SemaphoreType.DMA((2,)),
            pltpu.SemaphoreType.DMA((5,)),
            pltpu.SemaphoreType.DMA((5,)),
        ],
        compiler_params=pltpu.CompilerParams(collective_id=0, has_side_effects=True, vmem_limit_bytes=46 << 20),
        name="channelize_beams",
    )(delays, fir_coeffs, rows, weights, jnp.asarray(twiddle_table()))
    return power.reshape(PER, MLOC, BEAMS)


def solution(mesh):
    placed = (P("stn", None, None, "tm"), P("stn"), P(), P("stn", None, None, None))
    return jax.shard_map(
        per_device, mesh=mesh, in_specs=placed, out_specs=P("stn", "tm", None), check_vma=False
    )
```

```python
import math

import jax
import jax.numpy as jnp
import ml_dtypes
import numpy as np
from jax import lax
from jax.experimental import pallas as pl
from jax.experimental.pallas import tpu as pltpu
from jax.sharding import PartitionSpec as P

MESH = pl.DeviceIdType.MESH
BF, F32 = jnp.bfloat16, jnp.float32
CH, TAPS, BEAMS, DMAX = 1024, 16, 1024, 4096
PEERS = 32
LOCAL = 4
PER = CH // PEERS
MLOC = 128
HALF = MLOC // 2
FIRST = 16
LEAD = TAPS - 1
FRAMES = LEAD + MLOC + DMAX // CH
ROWS = FRAMES * 16 + 16
LEAD_ROWS, OWN_ROWS, TRAIL_ROWS = LEAD * 16, MLOC * 16, DMAX // CH * 16
FS = 136
XS = 136


def twiddle_table():
    n = np.arange(CH // 4)
    out = np.zeros((4, PEERS, PER // 4, 2, 2, CH // 4), np.float64)
    for r in range(4):
        k = PER * np.arange(PEERS)[:, None] + 4 * np.arange(PER // 4)[None, :] + r
        angle = 2 * np.pi * ((k[:, :, None] * n) % CH) / CH
        cosine, sine = np.cos(angle) / math.sqrt(CH), np.sin(angle) / math.sqrt(CH)
        out[r, :, :, 0, 0], out[r, :, :, 0, 1] = cosine, sine
        out[r, :, :, 1, 0], out[r, :, :, 1, 1] = -sine, cosine
    return out.reshape(4, CH // 2, CH // 2).astype(ml_dtypes.bfloat16)


def interleave(received, X):
    def body(g, carry):
        for s in range(LOCAL):
            X[pl.ds(g * LOCAL + s, 16, stride=XS), :] = received[g, s].astype(F32)
        return carry

    lax.fori_loop(0, PEERS, body, 0, unroll=2)


def beam(X, j, weights):
    rows = [pl.ds(pl.multiple_of((2 * j + c) * XS, 8), 128) for c in range(2)]
    re, im = [X[v, :].astype(BF).T for v in rows]
    lhs = jnp.concatenate([jnp.concatenate([re, -im], 1), jnp.concatenate([im, re], 1)], 0)
    y = jnp.dot(lhs, weights, preferred_element_type=F32)
    y = y * y
    power = (y[:HALF] + y[HALF : 2 * HALF]) + (y[2 * HALF : 3 * HALF] + y[3 * HALF :])
    return power.astype(BF)


def tail_kernel(done, R, W, out, X, O, done_sem, tail_sem):
    last = 3
    copies = [pltpu.make_async_copy(done.at[:, r], out.at[:, r], done_sem.at[r]) for r in range(last)]
    half = pl.ds(FIRST, HALF)
    copies.append(pltpu.make_async_copy(done.at[:, last, half], out.at[:, last, half], done_sem.at[last]))
    for copy in copies:
        copy.start()
    interleave(R.at[1, last], X)

    def body(j, carry):
        O[j] = beam(X, j, W[j, last])
        head = MLOC - FIRST - HALF
        pltpu.make_async_copy(O.at[j, pl.ds(0, head)], out.at[j, last, pl.ds(FIRST + HALF, head)], tail_sem).start()
        pltpu.make_async_copy(O.at[j, pl.ds(head, FIRST)], out.at[j, last, pl.ds(0, FIRST)], tail_sem).start()
        return carry

    lax.fori_loop(0, PER // 4, body, 0)
    for copy in copies:
        copy.wait()
    pltpu.make_async_copy(O, O, tail_sem).wait()


def kernel(delays, coef, base, weights, table, out, R, W, raw, E, C, Fq, F, T, S, X,
           base_sem, table_sem, weight_sem, halo_send, halo_recv, send_sem, recv_sem):
    t, me = lax.axis_index("tm"), lax.axis_index("stn")
    mz, my, mx = me // 16, (me // 4) % 4, me % 4

    def peer(i):
        q = (i * 13) % PEERS
        return ((mz + q // 16) % 2) * 16 + ((my + (q // 4) % 4) % 4) * 4 + (mx + q % 4) % 4

    def at(stn):
        return {"tm": t, "stn": stn}

    def base_copy(s):
        return pltpu.make_async_copy(base.at[s], raw.at[s, :, pl.ds(LEAD_ROWS, OWN_ROWS)], base_sem.at[s])

    base_copy(0).start()

    barrier = pltpu.get_barrier_semaphore()

    def greet(i, carry):
        pl.semaphore_signal(barrier, inc=1, device_id=at(peer(i)), device_id_type=MESH)
        return carry

    lax.fori_loop(1, PEERS, greet, 0)

    @pl.when(t > 0)
    def _():
        pl.semaphore_signal(barrier, inc=1, device_id={"tm": t - 1, "stn": me}, device_id_type=MESH)

    @pl.when(t < 3)
    def _():
        pl.semaphore_signal(barrier, inc=1, device_id={"tm": t + 1, "stn": me}, device_id_type=MESH)

    for s in range(1, LOCAL):
        base_copy(s).start()
    table_copy = pltpu.make_async_copy(table, T, table_sem)
    table_copy.start()
    weight_copy = pltpu.make_async_copy(weights, W, weight_sem)

    for k in range(TAPS):
        for j in range(8):
            pair = jnp.broadcast_to(coef[k : k + 1, 128 * j : 128 * j + 128], (2, 128))
            C[k, j // 4, 2 * (j % 4) : 2 * (j % 4) + 2, :] = pair
    raw[:, :, FRAMES * 16 :, :] = jnp.zeros((LOCAL, 2, 16, 128), BF)

    @pl.when(t == 0)
    def _():
        raw[:, :, :LEAD_ROWS, :] = jnp.zeros((LOCAL, 2, LEAD_ROWS, 128), BF)

    @pl.when(t == 3)
    def _():
        raw[:, :, LEAD_ROWS + OWN_ROWS : FRAMES * 16, :] = jnp.zeros((LOCAL, 2, TRAIL_ROWS, 128), BF)

    ahead = raw.at[:, :, pl.ds(0, LEAD_ROWS)], raw.at[:, :, pl.ds(LEAD_ROWS + OWN_ROWS, TRAIL_ROWS)]

    def send_halo(which):
        to = {"tm": t + 1 - 2 * which, "stn": me}

        parts = 5 if which == 0 else 1
        size = (LEAD_ROWS if which == 0 else TRAIL_ROWS) // parts
        start = OWN_ROWS - LEAD_ROWS if which == 0 else 0
        place = 0 if which == 0 else LEAD_ROWS + OWN_ROWS

        def body(i, carry):
            s, p = (i // 2) % LOCAL, i % 2
            at_row = pl.multiple_of(size * (i // (2 * LOCAL)), 16)
            pltpu.make_async_remote_copy(
                base.at[s, p, pl.ds(start + at_row, size)], raw.at[s, p, pl.ds(place + at_row, size)],
                halo_send.at[which], halo_recv.at[which], device_id=to, device_id_type=MESH).start()
            return carry

        lax.fori_loop(0, 2 * LOCAL * parts, body, 0)

    def halo_wait(sems, which):
        pltpu.make_async_copy(ahead[which], ahead[which], sems.at[which]).wait()

    def rotate(s, shift, first, count):
        j = lax.broadcasted_iota(jnp.int32, (128, 128), 0)
        lane = lax.broadcasted_iota(jnp.int32, (128, 128), 1)
        rotation = jnp.where((j == lane + shift) | (j == lane + shift - 128), 1.0, 0.0).astype(BF)

        def body(p, carry):
            rows = pl.ds(first * 16, count * 16)
            E[s, p, rows, :] = jnp.dot(raw[s, p, rows, :], rotation, preferred_element_type=F32)
            return carry

        lax.fori_loop(0, 2, body, 0)

    def fir(s, h, tiles, shift):
        keep = lax.broadcasted_iota(jnp.int32, (8, 128), 1) < 128 - shift

        def body(it, carry):
            i, p, half = it // 4, (it // 2) % 2, it % 2
            first = (FIRST + HALF * h + 16 * i) % MLOC
            d = []
            for f in range(31):
                row = (first + f) * 16 + half * 8 + 2 * tiles
                d.append(jnp.where(keep, E[s, p, pl.ds(row, 8), :], E[s, p, pl.ds(row + 2, 8), :]))
            for m in range(16):
                total = C[0, half] * d[m]
                for k in range(1, TAPS):
                    total = total + C[k, half] * d[m + k]
                Fq[pl.ds(half * 8 * FS + p * HALF + i * 16 + m, 8, stride=FS), :] = total
            return carry

        lax.fori_loop(0, 16, body, 0)

    def butterfly(place):
        def body(block, carry):
            rows = pl.multiple_of(block * 16, 16)
            for low in range(2):
                x = [[Fq[pl.ds(rows + ((2 * q + low) * 2 + c) * FS, 16), :] for q in range(4)] for c in range(2)]
                t0, t1 = [v[0] + v[2] for v in x], [v[0] - v[2] for v in x]
                t2, t3 = [v[1] + v[3] for v in x], [v[1] - v[3] for v in x]
                y = [
                    [t0[0] + t2[0], t0[1] + t2[1]],
                    [t1[0] + t3[1], t1[1] - t3[0]],
                    [t0[0] - t2[0], t0[1] - t2[1]],
                    [t1[0] - t3[1], t1[1] + t3[0]],
                ]
                for r in range(4):
                    for c in range(2):
                        lanes = c * 256 + low * 128
                        F[r, pl.ds(place * 128 + rows, 16), lanes : lanes + 128] = y[r][c].astype(BF)
            return carry

        lax.fori_loop(0, 8, body, 0)

    def transform(h, first, count):
        def body(r, carry):
            rows = F[r] if count == 2 else F[r, :128]
            spectra = lax.dot_general(T[r], rows, (((1,), (1,)), ((), ())), preferred_element_type=F32).astype(BF)
            for i in range(count):
                S[h, r, :, first + i] = spectra[:, 128 * i : 128 * i + 128].reshape(PEERS, 16, 128)
            return carry

        lax.fori_loop(0, 4, body, 0)

    def filtered(h, s, place):
        delay = delays[s]
        fir(s, h, delay // 128, delay % 128)
        butterfly(place)

    def send_first(s):
        def body(i, carry):
            d = peer(i)
            one = pl.ds(s, 1)
            pltpu.make_async_remote_copy(
                S.at[0, :, d, one], R.at[0, :, me, one], send_sem.at[0], recv_sem.at[0],
                device_id=at(d), device_id_type=MESH).start()
            return carry

        lax.fori_loop(1, PEERS, body, 0)

    def send_second(r):
        def body(i, carry):
            d = peer(i)
            pltpu.make_async_remote_copy(
                S.at[1, r, d], R.at[1, r, me], send_sem.at[1 + r], recv_sem.at[1 + r],
                device_id=at(d), device_id_type=MESH).start()
            return carry

        lax.fori_loop(1, PEERS, body, 0)
        pltpu.make_async_copy(S.at[1, r, me], R.at[1, r, me], recv_sem.at[1 + r]).start()

    def beams(h, r):
        interleave(R.at[h, r], X)

        def body(j, carry):
            power = beam(X, j, W[j, r])
            if h == 0:
                out[j, r, FIRST : FIRST + HALF, :] = power
            else:
                out[j, r, FIRST + HALF :, :] = power[: MLOC - FIRST - HALF]
                out[j, r, :FIRST, :] = power[MLOC - FIRST - HALF :]
            return carry

        lax.fori_loop(0, PER // 4, body, 0)

    pl.semaphore_wait(barrier, PEERS - 1 + (t + 2) // 3 + (5 - t) // 3)
    pl.when(t < 3)(lambda: send_halo(0))
    pl.when(t > 0)(lambda: send_halo(1))

    def first_rows(s):
        base_copy(s).wait()
        rotate(s, delays[s] % 128, 16, 84)

    first_rows(0)

    def first(s, carry):
        pl.when(s > 0)(lambda: first_rows(s))
        filtered(0, s, 0)
        pl.when(s == 0)(table_copy.wait)
        transform(0, s, 1)
        send_first(s)
        pl.when(s == 0)(weight_copy.start)
        return carry

    lax.fori_loop(0, LOCAL, first, 0)
    pltpu.make_async_copy(S.at[0, :, me], R.at[0, :, me], recv_sem.at[0]).start()
    pl.when(t > 0)(lambda: halo_wait(halo_recv, 0))
    pl.when(t < 3)(lambda: halo_wait(halo_recv, 1))

    def second(pair, carry):
        def body(i, carry):
            s = 2 * pair + i
            rotate(s, delays[s] % 128, 0, 16)
            rotate(s, delays[s] % 128, 100, 48)
            filtered(1, s, i)
            return carry

        lax.fori_loop(0, 2, body, 0)
        transform(1, 2 * pair, 2)
        return carry

    lax.fori_loop(0, 2, second, 0)
    send_second(0)
    weight_copy.wait()
    pltpu.make_async_copy(R.at[0], R.at[0], recv_sem.at[0]).wait()

    def finish_first(r, carry):
        pl.when(r < 3)(lambda: send_second(r + 1))
        beams(0, r)
        return carry

    lax.fori_loop(0, 4, finish_first, 0)

    def finish_second(r, carry):
        pltpu.make_async_copy(R.at[1, r], R.at[1, r], recv_sem.at[1 + r]).wait()
        pl.when(r < 3)(lambda: beams(1, r))
        return carry

    lax.fori_loop(0, 4, finish_second, 0)

    sent = pl.ds(0, PEERS - 1)
    pltpu.make_async_copy(S.at[0, :, sent], S.at[0, :, sent], send_sem.at[0]).wait()

    def sent_second(r, carry):
        pltpu.make_async_copy(S.at[1, r, sent], S.at[1, r, sent], send_sem.at[1 + r]).wait()
        return carry

    lax.fori_loop(0, 4, sent_second, 0)

    pl.when(t < 3)(lambda: halo_wait(halo_send, 0))
    pl.when(t > 0)(lambda: halo_wait(halo_send, 1))


def per_device(baseband, delays, fir_coeffs, beam_weights):
    rows = baseband.reshape(LOCAL, 2, 2, OWN_ROWS // 2, 128).transpose(0, 1, 3, 2, 4).reshape(LOCAL, 2, OWN_ROWS, 128)
    weights = beam_weights.reshape(PER // 4, 4, 2 * LOCAL * PEERS, BEAMS)
    anywhere = pl.BlockSpec(memory_space=pl.ANY)
    whole = pl.BlockSpec(memory_space=pltpu.VMEM)
    done, received, held = pl.pallas_call(
        kernel,
        out_shape=(
            pltpu.VMEM((PER // 4, 4, MLOC, BEAMS), BF),
            pltpu.VMEM((2, 4, PEERS, LOCAL, 16, 128), BF),
            pltpu.VMEM((PER // 4, 4, 2 * LOCAL * PEERS, BEAMS), BF),
        ),
        in_specs=[pl.BlockSpec(memory_space=pltpu.SMEM), pl.BlockSpec(memory_space=pltpu.VMEM), anywhere, anywhere, anywhere],
        out_specs=(whole, whole, whole),
        scratch_shapes=[
            pltpu.VMEM((LOCAL, 2, ROWS, 128), BF),
            pltpu.VMEM((LOCAL, 2, ROWS, 128), F32),
            pltpu.VMEM((TAPS, 2, 8, 128), F32),
            pltpu.VMEM((16 * FS, 128), F32),
            pltpu.VMEM((4, 256, CH // 2), BF),
            pltpu.VMEM((4, CH // 2, CH // 2), BF),
            pltpu.VMEM((2, 4, PEERS, LOCAL, 16, 128), BF),
            pltpu.VMEM((16 * XS, 128), F32),
            pltpu.SemaphoreType.DMA((LOCAL,)),
            pltpu.SemaphoreType.DMA,
            pltpu.SemaphoreType.DMA,
            pltpu.SemaphoreType.DMA((2,)),
            pltpu.SemaphoreType.DMA((2,)),
            pltpu.SemaphoreType.DMA((5,)),
            pltpu.SemaphoreType.DMA((5,)),
        ],
        compiler_params=pltpu.CompilerParams(collective_id=0, has_side_effects=True, vmem_limit_bytes=26 << 20),
        name="channelize_beams",
    )(delays, fir_coeffs, rows, weights, jnp.asarray(twiddle_table()))
    power = pl.pallas_call(
        tail_kernel,
        out_shape=jax.ShapeDtypeStruct((PER // 4, 4, MLOC, BEAMS), BF),
        in_specs=[whole, whole, whole],
        out_specs=anywhere,
        scratch_shapes=[
            pltpu.VMEM((16 * XS, 128), F32),
            pltpu.VMEM((PER // 4, HALF, BEAMS), BF),
            pltpu.SemaphoreType.DMA((4,)),
            pltpu.SemaphoreType.DMA,
        ],
        compiler_params=pltpu.CompilerParams(vmem_limit_bytes=8 << 20),
        name="tail_beams",
    )(*[pltpu.with_memory_space_constraint(v, pltpu.VMEM) for v in (done, received, held)])
    return power.reshape(PER, MLOC, BEAMS)


def solution(mesh):
    placed = (P("stn", None, None, "tm"), P("stn"), P(), P("stn", None, None, None))
    return jax.shard_map(
        per_device, mesh=mesh, in_specs=placed, out_specs=P("stn", "tm", None), check_vma=False
    )
```

```python
import math

import jax
import jax.numpy as jnp
import ml_dtypes
import numpy as np
from jax import lax
from jax.experimental import pallas as pl
from jax.experimental.pallas import tpu as pltpu
from jax.sharding import PartitionSpec as P

MESH = pl.DeviceIdType.MESH
BF, F32 = jnp.bfloat16, jnp.float32
CH, TAPS, BEAMS, DMAX = 1024, 16, 1024, 4096
PEERS = 32
LOCAL = 4
PER = CH // PEERS
MLOC = 128
HALF = MLOC // 2
FIRST = 16
LEAD = TAPS - 1
FRAMES = LEAD + MLOC + DMAX // CH
ROWS = FRAMES * 16 + 16
LEAD_ROWS, OWN_ROWS, TRAIL_ROWS = LEAD * 16, MLOC * 16, DMAX // CH * 16
FS = 136
XS = 136


def twiddle_table():
    n = np.arange(CH // 4)
    out = np.zeros((4, PEERS, PER // 4, 2, 2, CH // 4), np.float64)
    for r in range(4):
        k = PER * np.arange(PEERS)[:, None] + 4 * np.arange(PER // 4)[None, :] + r
        angle = 2 * np.pi * ((k[:, :, None] * n) % CH) / CH
        cosine, sine = np.cos(angle) / math.sqrt(CH), np.sin(angle) / math.sqrt(CH)
        out[r, :, :, 0, 0], out[r, :, :, 0, 1] = cosine, sine
        out[r, :, :, 1, 0], out[r, :, :, 1, 1] = -sine, cosine
    return out.reshape(4, CH // 2, CH // 2).astype(ml_dtypes.bfloat16)


def interleave(received, X):
    def body(g, carry):
        for s in range(LOCAL):
            X[pl.ds(g * LOCAL + s, 16, stride=XS), :] = received[g, s].astype(F32)
        return carry

    lax.fori_loop(0, PEERS, body, 0, unroll=2)


def beam(X, j, weights):
    rows = [pl.ds(pl.multiple_of((2 * j + c) * XS, 8), 128) for c in range(2)]
    re, im = [X[v, :].astype(BF).T for v in rows]
    lhs = jnp.concatenate([jnp.concatenate([re, -im], 1), jnp.concatenate([im, re], 1)], 0)
    y = jnp.dot(lhs, weights, preferred_element_type=F32)
    y = y * y
    power = (y[:HALF] + y[HALF : 2 * HALF]) + (y[2 * HALF : 3 * HALF] + y[3 * HALF :])
    return power.astype(BF)


def tail_kernel(done, R, W, out, X, O, done_sem, tail_sem):
    last = 3
    copies = [pltpu.make_async_copy(done.at[:, r], out.at[:, r], done_sem.at[r]) for r in range(last)]
    half = pl.ds(FIRST, HALF)
    copies.append(pltpu.make_async_copy(done.at[:, last, half], out.at[:, last, half], done_sem.at[last]))
    for copy in copies:
        copy.start()
    interleave(R.at[1, last], X)

    def body(j, carry):
        O[j] = beam(X, j, W[j, last])
        head = MLOC - FIRST - HALF
        pltpu.make_async_copy(O.at[j, pl.ds(0, head)], out.at[j, last, pl.ds(FIRST + HALF, head)], tail_sem).start()
        pltpu.make_async_copy(O.at[j, pl.ds(head, FIRST)], out.at[j, last, pl.ds(0, FIRST)], tail_sem).start()
        return carry

    lax.fori_loop(0, PER // 4, body, 0)
    for copy in copies:
        copy.wait()
    pltpu.make_async_copy(O, O, tail_sem).wait()


def kernel(delays, coef, base, weights, table, out, R, W, raw, E, C, Fq, F, T, S, X,
           base_sem, table_sem, weight_sem, halo_send, halo_recv, send_sem, recv_sem):
    t, me = lax.axis_index("tm"), lax.axis_index("stn")
    mz, my, mx = me // 16, (me // 4) % 4, me % 4

    def peer(i):
        q = (i * 13) % PEERS
        return ((mz + q // 16) % 2) * 16 + ((my + (q // 4) % 4) % 4) * 4 + (mx + q % 4) % 4

    def at(stn):
        return {"tm": t, "stn": stn}

    def base_copy(s):
        return pltpu.make_async_copy(base.at[s], raw.at[s, :, pl.ds(LEAD_ROWS, OWN_ROWS)], base_sem.at[s])

    base_copy(0).start()

    barrier = pltpu.get_barrier_semaphore()

    def greet(i, carry):
        pl.semaphore_signal(barrier, inc=1, device_id=at(peer(i)), device_id_type=MESH)
        return carry

    lax.fori_loop(1, PEERS, greet, 0)

    @pl.when(t > 0)
    def _():
        pl.semaphore_signal(barrier, inc=1, device_id={"tm": t - 1, "stn": me}, device_id_type=MESH)

    @pl.when(t < 3)
    def _():
        pl.semaphore_signal(barrier, inc=1, device_id={"tm": t + 1, "stn": me}, device_id_type=MESH)

    for s in range(1, LOCAL):
        base_copy(s).start()
    table_copy = pltpu.make_async_copy(table, T, table_sem)
    table_copy.start()
    weight_copy = pltpu.make_async_copy(weights, W, weight_sem)

    for k in range(TAPS):
        for j in range(8):
            pair = jnp.broadcast_to(coef[k : k + 1, 128 * j : 128 * j + 128], (2, 128))
            C[k, j // 4, 2 * (j % 4) : 2 * (j % 4) + 2, :] = pair
    raw[:, :, FRAMES * 16 :, :] = jnp.zeros((LOCAL, 2, 16, 128), BF)

    @pl.when(t == 0)
    def _():
        raw[:, :, :LEAD_ROWS, :] = jnp.zeros((LOCAL, 2, LEAD_ROWS, 128), BF)

    @pl.when(t == 3)
    def _():
        raw[:, :, LEAD_ROWS + OWN_ROWS : FRAMES * 16, :] = jnp.zeros((LOCAL, 2, TRAIL_ROWS, 128), BF)

    ahead = raw.at[:, :, pl.ds(0, LEAD_ROWS)], raw.at[:, :, pl.ds(LEAD_ROWS + OWN_ROWS, TRAIL_ROWS)]

    def send_halo(which):
        to = {"tm": t + 1 - 2 * which, "stn": me}

        parts = 5 if which == 0 else 1
        size = (LEAD_ROWS if which == 0 else TRAIL_ROWS) // parts
        start = OWN_ROWS - LEAD_ROWS if which == 0 else 0
        place = 0 if which == 0 else LEAD_ROWS + OWN_ROWS

        def body(i, carry):
            s, p = (i // 2) % LOCAL, i % 2
            at_row = pl.multiple_of(size * (i // (2 * LOCAL)), 16)
            pltpu.make_async_remote_copy(
                base.at[s, p, pl.ds(start + at_row, size)], raw.at[s, p, pl.ds(place + at_row, size)],
                halo_send.at[which], halo_recv.at[which], device_id=to, device_id_type=MESH).start()
            return carry

        lax.fori_loop(0, 2 * LOCAL * parts, body, 0)

    def halo_wait(sems, which):
        pltpu.make_async_copy(ahead[which], ahead[which], sems.at[which]).wait()

    def rotate(s, shift, first, count):
        j = lax.broadcasted_iota(jnp.int32, (128, 128), 0)
        lane = lax.broadcasted_iota(jnp.int32, (128, 128), 1)
        rotation = jnp.where((j == lane + shift) | (j == lane + shift - 128), 1.0, 0.0).astype(BF)

        def body(p, carry):
            rows = pl.ds(first * 16, count * 16)
            E[s, p, rows, :] = jnp.dot(raw[s, p, rows, :], rotation, preferred_element_type=F32)
            return carry

        lax.fori_loop(0, 2, body, 0)

    def fir(s, h, tiles, shift):
        keep = lax.broadcasted_iota(jnp.int32, (8, 128), 1) < 128 - shift

        def body(it, carry):
            i, p, half = it // 4, (it // 2) % 2, it % 2
            first = (FIRST + HALF * h + 16 * i) % MLOC
            d = []
            for f in range(31):
                row = (first + f) * 16 + half * 8 + 2 * tiles
                d.append(jnp.where(keep, E[s, p, pl.ds(row, 8), :], E[s, p, pl.ds(row + 2, 8), :]))
            for m in range(16):
                total = C[0, half] * d[m]
                for k in range(1, TAPS):
                    total = total + C[k, half] * d[m + k]
                Fq[pl.ds(half * 8 * FS + p * HALF + i * 16 + m, 8, stride=FS), :] = total
            return carry

        lax.fori_loop(0, 16, body, 0)

    def butterfly(place):
        def body(block, carry):
            rows = pl.multiple_of(block * 16, 16)
            for low in range(2):
                x = [[Fq[pl.ds(rows + ((2 * q + low) * 2 + c) * FS, 16), :] for q in range(4)] for c in range(2)]
                t0, t1 = [v[0] + v[2] for v in x], [v[0] - v[2] for v in x]
                t2, t3 = [v[1] + v[3] for v in x], [v[1] - v[3] for v in x]
                y = [
                    [t0[0] + t2[0], t0[1] + t2[1]],
                    [t1[0] + t3[1], t1[1] - t3[0]],
                    [t0[0] - t2[0], t0[1] - t2[1]],
                    [t1[0] - t3[1], t1[1] + t3[0]],
                ]
                for r in range(4):
                    for c in range(2):
                        lanes = c * 256 + low * 128
                        F[r, pl.ds(place * 128 + rows, 16), lanes : lanes + 128] = y[r][c].astype(BF)
            return carry

        lax.fori_loop(0, 8, body, 0)

    def transform(h, first, count):
        def body(r, carry):
            rows = F[r] if count == 2 else F[r, :128]
            spectra = lax.dot_general(T[r], rows, (((1,), (1,)), ((), ())), preferred_element_type=F32).astype(BF)
            for i in range(count):
                S[h, r, :, first + i] = spectra[:, 128 * i : 128 * i + 128].reshape(PEERS, 16, 128)
            return carry

        lax.fori_loop(0, 4, body, 0)

    def filtered(h, s, place):
        delay = delays[s]
        fir(s, h, delay // 128, delay % 128)
        butterfly(place)

    def send_first(s, count):
        def body(i, carry):
            d = peer(i)
            one = pl.ds(s, count)
            pltpu.make_async_remote_copy(
                S.at[0, :, d, one], R.at[0, :, me, one], send_sem.at[0], recv_sem.at[0],
                device_id=at(d), device_id_type=MESH).start()
            return carry

        lax.fori_loop(1, PEERS, body, 0, unroll=PEERS - 1)

    def send_second(r):
        def body(i, carry):
            d = peer(i)
            pltpu.make_async_remote_copy(
                S.at[1, r, d], R.at[1, r, me], send_sem.at[1 + r], recv_sem.at[1 + r],
                device_id=at(d), device_id_type=MESH).start()
            return carry

        lax.fori_loop(1, PEERS, body, 0, unroll=PEERS - 1)
        pltpu.make_async_copy(S.at[1, r, me], R.at[1, r, me], recv_sem.at[1 + r]).start()

    def beams(h, r):
        interleave(R.at[h, r], X)

        def body(j, carry):
            power = beam(X, j, W[j, r])
            if h == 0:
                out[j, r, FIRST : FIRST + HALF, :] = power
            else:
                out[j, r, FIRST + HALF :, :] = power[: MLOC - FIRST - HALF]
                out[j, r, :FIRST, :] = power[MLOC - FIRST - HALF :]
            return carry

        lax.fori_loop(0, PER // 4, body, 0)

    pl.semaphore_wait(barrier, PEERS - 1 + (t + 2) // 3 + (5 - t) // 3)
    pl.when(t < 3)(lambda: send_halo(0))
    pl.when(t > 0)(lambda: send_halo(1))

    def first_rows(s):
        base_copy(s).wait()
        rotate(s, delays[s] % 128, 16, 84)

    first_rows(0)

    def first(s, carry):
        pl.when(s > 0)(lambda: first_rows(s))
        filtered(0, s, 0)
        pl.when(s == 0)(table_copy.wait)
        transform(0, s, 1)
        send_first(s, 1)
        pl.when(s == 0)(weight_copy.start)
        return carry

    lax.fori_loop(0, 2, first, 0)

    def both(i, carry):
        first_rows(2 + i)
        filtered(0, 2 + i, i)
        return carry

    lax.fori_loop(0, 2, both, 0)
    transform(0, 2, 2)
    send_first(2, 2)
    pltpu.make_async_copy(S.at[0, :, me], R.at[0, :, me], recv_sem.at[0]).start()
    pl.when(t > 0)(lambda: halo_wait(halo_recv, 0))
    pl.when(t < 3)(lambda: halo_wait(halo_recv, 1))

    def second(pair, carry):
        def body(i, carry):
            s = 2 * pair + i
            rotate(s, delays[s] % 128, 0, 16)
            rotate(s, delays[s] % 128, 100, 48)
            filtered(1, s, i)
            return carry

        lax.fori_loop(0, 2, body, 0)
        transform(1, 2 * pair, 2)
        return carry

    lax.fori_loop(0, 2, second, 0)
    send_second(0)
    weight_copy.wait()
    pltpu.make_async_copy(R.at[0], R.at[0], recv_sem.at[0]).wait()

    def finish_first(r, carry):
        pl.when(r < 3)(lambda: send_second(r + 1))
        beams(0, r)
        return carry

    lax.fori_loop(0, 4, finish_first, 0)

    def finish_second(r, carry):
        pltpu.make_async_copy(R.at[1, r], R.at[1, r], recv_sem.at[1 + r]).wait()
        pl.when(r < 3)(lambda: beams(1, r))
        return carry

    lax.fori_loop(0, 4, finish_second, 0)

    sent = pl.ds(0, PEERS - 1)
    pltpu.make_async_copy(S.at[0, :, sent], S.at[0, :, sent], send_sem.at[0]).wait()

    def sent_second(r, carry):
        pltpu.make_async_copy(S.at[1, r, sent], S.at[1, r, sent], send_sem.at[1 + r]).wait()
        return carry

    lax.fori_loop(0, 4, sent_second, 0)

    pl.when(t < 3)(lambda: halo_wait(halo_send, 0))
    pl.when(t > 0)(lambda: halo_wait(halo_send, 1))


def per_device(baseband, delays, fir_coeffs, beam_weights):
    rows = baseband.reshape(LOCAL, 2, 2, OWN_ROWS // 2, 128).transpose(0, 1, 3, 2, 4).reshape(LOCAL, 2, OWN_ROWS, 128)
    weights = beam_weights.reshape(PER // 4, 4, 2 * LOCAL * PEERS, BEAMS)
    anywhere = pl.BlockSpec(memory_space=pl.ANY)
    whole = pl.BlockSpec(memory_space=pltpu.VMEM)
    done, received, held = pl.pallas_call(
        kernel,
        out_shape=(
            pltpu.VMEM((PER // 4, 4, MLOC, BEAMS), BF),
            pltpu.VMEM((2, 4, PEERS, LOCAL, 16, 128), BF),
            pltpu.VMEM((PER // 4, 4, 2 * LOCAL * PEERS, BEAMS), BF),
        ),
        in_specs=[pl.BlockSpec(memory_space=pltpu.SMEM), pl.BlockSpec(memory_space=pltpu.VMEM), anywhere, anywhere, anywhere],
        out_specs=(whole, whole, whole),
        scratch_shapes=[
            pltpu.VMEM((LOCAL, 2, ROWS, 128), BF),
            pltpu.VMEM((LOCAL, 2, ROWS, 128), F32),
            pltpu.VMEM((TAPS, 2, 8, 128), F32),
            pltpu.VMEM((16 * FS, 128), F32),
            pltpu.VMEM((4, 256, CH // 2), BF),
            pltpu.VMEM((4, CH // 2, CH // 2), BF),
            pltpu.VMEM((2, 4, PEERS, LOCAL, 16, 128), BF),
            pltpu.VMEM((16 * XS, 128), F32),
            pltpu.SemaphoreType.DMA((LOCAL,)),
            pltpu.SemaphoreType.DMA,
            pltpu.SemaphoreType.DMA,
            pltpu.SemaphoreType.DMA((2,)),
            pltpu.SemaphoreType.DMA((2,)),
            pltpu.SemaphoreType.DMA((5,)),
            pltpu.SemaphoreType.DMA((5,)),
        ],
        compiler_params=pltpu.CompilerParams(collective_id=0, has_side_effects=True, vmem_limit_bytes=26 << 20),
        name="channelize_beams",
    )(delays, fir_coeffs, rows, weights, jnp.asarray(twiddle_table()))
    power = pl.pallas_call(
        tail_kernel,
        out_shape=jax.ShapeDtypeStruct((PER // 4, 4, MLOC, BEAMS), BF),
        in_specs=[whole, whole, whole],
        out_specs=anywhere,
        scratch_shapes=[
            pltpu.VMEM((16 * XS, 128), F32),
            pltpu.VMEM((PER // 4, HALF, BEAMS), BF),
            pltpu.SemaphoreType.DMA((4,)),
            pltpu.SemaphoreType.DMA,
        ],
        compiler_params=pltpu.CompilerParams(vmem_limit_bytes=8 << 20),
        name="tail_beams",
    )(*[pltpu.with_memory_space_constraint(v, pltpu.VMEM) for v in (done, received, held)])
    return power.reshape(PER, MLOC, BEAMS)


def solution(mesh):
    placed = (P("stn", None, None, "tm"), P("stn"), P(), P("stn", None, None, None))
    return jax.shard_map(
        per_device, mesh=mesh, in_specs=placed, out_specs=P("stn", "tm", None), check_vma=False
    )
```

```python
import math

import jax
import jax.numpy as jnp
import ml_dtypes
import numpy as np
from jax import lax
from jax.experimental import pallas as pl
from jax.experimental.pallas import tpu as pltpu
from jax.sharding import PartitionSpec as P

MESH = pl.DeviceIdType.MESH
BF, F32 = jnp.bfloat16, jnp.float32
CH, TAPS, BEAMS, DMAX = 1024, 16, 1024, 4096
PEERS = 32
LOCAL = 4
PER = CH // PEERS
MLOC = 128
HALF = MLOC // 2
FIRST = 16
LEAD = TAPS - 1
FRAMES = LEAD + MLOC + DMAX // CH
ROWS = FRAMES * 16 + 16
LEAD_ROWS, OWN_ROWS, TRAIL_ROWS = LEAD * 16, MLOC * 16, DMAX // CH * 16
FS = 136
XS = 136


def twiddle_table():
    n = np.arange(CH // 4)
    out = np.zeros((4, PEERS, PER // 4, 2, 2, CH // 4), np.float64)
    for r in range(4):
        k = PER * np.arange(PEERS)[:, None] + 4 * np.arange(PER // 4)[None, :] + r
        angle = 2 * np.pi * ((k[:, :, None] * n) % CH) / CH
        cosine, sine = np.cos(angle) / math.sqrt(CH), np.sin(angle) / math.sqrt(CH)
        out[r, :, :, 0, 0], out[r, :, :, 0, 1] = cosine, sine
        out[r, :, :, 1, 0], out[r, :, :, 1, 1] = -sine, cosine
    return out.reshape(4, CH // 2, CH // 2).astype(ml_dtypes.bfloat16)


def interleave(received, X):
    def body(g, carry):
        for s in range(LOCAL):
            X[pl.ds(g * LOCAL + s, 16, stride=XS), :] = received[g, s].astype(F32)
        return carry

    lax.fori_loop(0, PEERS, body, 0, unroll=4)


def beam(X, j, weights):
    rows = [pl.ds(pl.multiple_of((2 * j + c) * XS, 8), 128) for c in range(2)]
    re, im = [X[v, :].astype(BF).T for v in rows]
    lhs = jnp.concatenate([jnp.concatenate([re, -im], 1), jnp.concatenate([im, re], 1)], 0)
    y = jnp.dot(lhs, weights, preferred_element_type=F32)
    y = y * y
    power = (y[:HALF] + y[HALF : 2 * HALF]) + (y[2 * HALF : 3 * HALF] + y[3 * HALF :])
    return power.astype(BF)


def tail_kernel(done, R, W, out, X, O, done_sem, tail_sem):
    last = 3
    copies = [pltpu.make_async_copy(done.at[:, r], out.at[:, r], done_sem.at[r]) for r in range(last)]
    half = pl.ds(FIRST, HALF)
    copies.append(pltpu.make_async_copy(done.at[:, last, half], out.at[:, last, half], done_sem.at[last]))
    for copy in copies:
        copy.start()
    interleave(R.at[1, last], X)

    def body(j, carry):
        O[j] = beam(X, j, W[j, last])
        head = MLOC - FIRST - HALF
        pltpu.make_async_copy(O.at[j, pl.ds(0, head)], out.at[j, last, pl.ds(FIRST + HALF, head)], tail_sem).start()
        pltpu.make_async_copy(O.at[j, pl.ds(head, FIRST)], out.at[j, last, pl.ds(0, FIRST)], tail_sem).start()
        return carry

    lax.fori_loop(0, PER // 4, body, 0, unroll=2)
    for copy in copies:
        copy.wait()
    pltpu.make_async_copy(O, O, tail_sem).wait()


def kernel(delays, coef, base, weights, table, out, R, W, raw, E, C, Fq, F, T, S, X,
           base_sem, table_sem, weight_sem, halo_send, halo_recv, send_sem, recv_sem):
    t, me = lax.axis_index("tm"), lax.axis_index("stn")
    mz, my, mx = me // 16, (me // 4) % 4, me % 4

    planes = [lax.rem(mz + i, 2) * 16 for i in range(2)]
    lines = [lax.rem(my + i, 4) * 4 for i in range(4)]
    columns = [lax.rem(mx + i, 4) for i in range(4)]

    def peer(i):
        q = (i * 13) % PEERS
        return planes[q // 16] + lines[(q // 4) % 4] + columns[q % 4]

    def at(stn):
        return {"tm": t, "stn": stn}

    def base_copy(s):
        return pltpu.make_async_copy(base.at[s], raw.at[s, :, pl.ds(LEAD_ROWS, OWN_ROWS)], base_sem.at[s])

    base_copy(0).start()

    barrier = pltpu.get_barrier_semaphore()

    def greet(i, carry):
        pl.semaphore_signal(barrier, inc=1, device_id=at(peer(i)), device_id_type=MESH)
        return carry

    for i in range(1, PEERS):
        greet(i, 0)

    @pl.when(t > 0)
    def _():
        pl.semaphore_signal(barrier, inc=1, device_id={"tm": t - 1, "stn": me}, device_id_type=MESH)

    @pl.when(t < 3)
    def _():
        pl.semaphore_signal(barrier, inc=1, device_id={"tm": t + 1, "stn": me}, device_id_type=MESH)

    for s in range(1, LOCAL):
        base_copy(s).start()
    table_copy = pltpu.make_async_copy(table, T, table_sem)
    table_copy.start()
    weight_copy = pltpu.make_async_copy(weights, W, weight_sem)

    ahead = raw.at[:, :, pl.ds(0, LEAD_ROWS)], raw.at[:, :, pl.ds(LEAD_ROWS + OWN_ROWS, TRAIL_ROWS)]

    def send_halo(which):
        to = {"tm": t + 1 - 2 * which, "stn": me}

        parts = 5 if which == 0 else 1
        size = (LEAD_ROWS if which == 0 else TRAIL_ROWS) // parts
        start = OWN_ROWS - LEAD_ROWS if which == 0 else 0
        place = 0 if which == 0 else LEAD_ROWS + OWN_ROWS

        def body(i, carry):
            s, p = (i // 2) % LOCAL, i % 2
            at_row = pl.multiple_of(size * (i // (2 * LOCAL)), 16)
            pltpu.make_async_remote_copy(
                base.at[s, p, pl.ds(start + at_row, size)], raw.at[s, p, pl.ds(place + at_row, size)],
                halo_send.at[which], halo_recv.at[which], device_id=to, device_id_type=MESH).start()
            return carry

        lax.fori_loop(0, 2 * LOCAL * parts, body, 0)

    def halo_wait(sems, which):
        pltpu.make_async_copy(ahead[which], ahead[which], sems.at[which]).wait()

    def rotate(s, shift, first, count):
        j = lax.broadcasted_iota(jnp.int32, (128, 128), 0)
        lane = lax.broadcasted_iota(jnp.int32, (128, 128), 1)
        rotation = jnp.where((j == lane + shift) | (j == lane + shift - 128), 1.0, 0.0).astype(BF)

        def body(p, carry):
            rows = pl.ds(first * 16, count * 16)
            E[s, p, rows, :] = jnp.dot(raw[s, p, rows, :], rotation, preferred_element_type=F32)
            return carry

        lax.fori_loop(0, 2, body, 0)

    def fir(s, h, tiles, shift):
        keep = lax.broadcasted_iota(jnp.int32, (8, 128), 1) < 128 - shift

        def body(it, carry):
            i, p, half = it // 4, (it // 2) % 2, it % 2
            first = (FIRST + HALF * h + 16 * i) % MLOC
            d = []
            for f in range(31):
                row = (first + f) * 16 + half * 8 + 2 * tiles
                d.append(jnp.where(keep, E[s, p, pl.ds(row, 8), :], E[s, p, pl.ds(row + 2, 8), :]))
            for m in range(16):
                total = C[0, half] * d[m]
                for k in range(1, TAPS):
                    total = total + C[k, half] * d[m + k]
                Fq[pl.ds(half * 8 * FS + p * HALF + i * 16 + m, 8, stride=FS), :] = total
            return carry

        lax.fori_loop(0, 16, body, 0)

    def butterfly(place):
        def body(block, carry):
            rows = pl.multiple_of(block * 16, 16)
            for low in range(2):
                x = [[Fq[pl.ds(rows + ((2 * q + low) * 2 + c) * FS, 16), :] for q in range(4)] for c in range(2)]
                t0, t1 = [v[0] + v[2] for v in x], [v[0] - v[2] for v in x]
                t2, t3 = [v[1] + v[3] for v in x], [v[1] - v[3] for v in x]
                y = [
                    [t0[0] + t2[0], t0[1] + t2[1]],
                    [t1[0] + t3[1], t1[1] - t3[0]],
                    [t0[0] - t2[0], t0[1] - t2[1]],
                    [t1[0] - t3[1], t1[1] + t3[0]],
                ]
                for r in range(4):
                    for c in range(2):
                        lanes = c * 256 + low * 128
                        F[r, pl.ds(place * 128 + rows, 16), lanes : lanes + 128] = y[r][c].astype(BF)
            return carry

        lax.fori_loop(0, 8, body, 0)

    def transform(h, first, count):
        def body(r, carry):
            rows = F[r] if count == 2 else F[r, :128]
            spectra = lax.dot_general(T[r], rows, (((1,), (1,)), ((), ())), preferred_element_type=F32).astype(BF)
            for i in range(count):
                S[h, r, :, first + i] = spectra[:, 128 * i : 128 * i + 128].reshape(PEERS, 16, 128)
            return carry

        lax.fori_loop(0, 4, body, 0)

    def filtered(h, s, place):
        delay = delays[s]
        fir(s, h, delay // 128, delay % 128)
        butterfly(place)

    def send_first(s, count):
        def body(i, carry):
            d = peer(i)
            one = pl.ds(s, count)
            pltpu.make_async_remote_copy(
                S.at[0, :, d, one], R.at[0, :, me, one], send_sem.at[0], recv_sem.at[0],
                device_id=at(d), device_id_type=MESH).start()
            return carry

        for i in range(1, PEERS):
            body(i, 0)

    def send_second(r):
        def body(i, carry):
            d = peer(i)
            pltpu.make_async_remote_copy(
                S.at[1, r, d], R.at[1, r, me], send_sem.at[1 + r], recv_sem.at[1 + r],
                device_id=at(d), device_id_type=MESH).start()
            return carry

        for i in range(1, PEERS):
            body(i, 0)
        pltpu.make_async_copy(S.at[1, r, me], R.at[1, r, me], recv_sem.at[1 + r]).start()

    def beams(h, r):
        interleave(R.at[h, r], X)

        def body(j, carry):
            power = beam(X, j, W[j, r])
            if h == 0:
                out[j, r, FIRST : FIRST + HALF, :] = power
            else:
                out[j, r, FIRST + HALF :, :] = power[: MLOC - FIRST - HALF]
                out[j, r, :FIRST, :] = power[MLOC - FIRST - HALF :]
            return carry

        lax.fori_loop(0, PER // 4, body, 0, unroll=2)

    pl.semaphore_wait(barrier, PEERS - 1 + (t + 2) // 3 + (5 - t) // 3)
    pl.when(t < 3)(lambda: send_halo(0))
    pl.when(t > 0)(lambda: send_halo(1))

    for k in range(TAPS):
        for j in range(8):
            pair = jnp.broadcast_to(coef[k : k + 1, 128 * j : 128 * j + 128], (2, 128))
            C[k, j // 4, 2 * (j % 4) : 2 * (j % 4) + 2, :] = pair
    raw[:, :, FRAMES * 16 :, :] = jnp.zeros((LOCAL, 2, 16, 128), BF)

    @pl.when(t == 0)
    def _():
        raw[:, :, :LEAD_ROWS, :] = jnp.zeros((LOCAL, 2, LEAD_ROWS, 128), BF)

    @pl.when(t == 3)
    def _():
        raw[:, :, LEAD_ROWS + OWN_ROWS : FRAMES * 16, :] = jnp.zeros((LOCAL, 2, TRAIL_ROWS, 128), BF)

    def first_rows(s):
        base_copy(s).wait()
        rotate(s, delays[s] % 128, 16, 84)

    first_rows(0)

    def first(s, carry):
        pl.when(s > 0)(lambda: first_rows(s))
        filtered(0, s, 0)
        pl.when(s == 0)(table_copy.wait)
        transform(0, s, 1)
        send_first(s, 1)
        pl.when(s == 0)(weight_copy.start)
        return carry

    lax.fori_loop(0, 2, first, 0)

    def both(i, carry):
        first_rows(2 + i)
        filtered(0, 2 + i, i)
        return carry

    lax.fori_loop(0, 2, both, 0)
    transform(0, 2, 2)
    send_first(2, 2)
    pltpu.make_async_copy(S.at[0, :, me], R.at[0, :, me], recv_sem.at[0]).start()
    pl.when(t > 0)(lambda: halo_wait(halo_recv, 0))
    pl.when(t < 3)(lambda: halo_wait(halo_recv, 1))

    def second(pair, carry):
        def body(i, carry):
            s = 2 * pair + i
            rotate(s, delays[s] % 128, 0, 16)
            rotate(s, delays[s] % 128, 100, 48)
            filtered(1, s, i)
            return carry

        lax.fori_loop(0, 2, body, 0)
        transform(1, 2 * pair, 2)
        return carry

    lax.fori_loop(0, 2, second, 0)
    send_second(0)
    weight_copy.wait()
    pltpu.make_async_copy(R.at[0], R.at[0], recv_sem.at[0]).wait()

    def finish_first(r, carry):
        pl.when(r < 3)(lambda: send_second(r + 1))
        beams(0, r)
        return carry

    lax.fori_loop(0, 4, finish_first, 0)

    def finish_second(r, carry):
        pltpu.make_async_copy(R.at[1, r], R.at[1, r], recv_sem.at[1 + r]).wait()
        pl.when(r < 3)(lambda: beams(1, r))
        return carry

    lax.fori_loop(0, 4, finish_second, 0)

    sent = pl.ds(0, PEERS - 1)
    pltpu.make_async_copy(S.at[0, :, sent], S.at[0, :, sent], send_sem.at[0]).wait()

    def sent_second(r, carry):
        pltpu.make_async_copy(S.at[1, r, sent], S.at[1, r, sent], send_sem.at[1 + r]).wait()
        return carry

    lax.fori_loop(0, 4, sent_second, 0)

    pl.when(t < 3)(lambda: halo_wait(halo_send, 0))
    pl.when(t > 0)(lambda: halo_wait(halo_send, 1))


def per_device(baseband, delays, fir_coeffs, beam_weights):
    rows = baseband.reshape(LOCAL, 2, 2, OWN_ROWS // 2, 128).transpose(0, 1, 3, 2, 4).reshape(LOCAL, 2, OWN_ROWS, 128)
    weights = beam_weights.reshape(PER // 4, 4, 2 * LOCAL * PEERS, BEAMS)
    anywhere = pl.BlockSpec(memory_space=pl.ANY)
    whole = pl.BlockSpec(memory_space=pltpu.VMEM)
    done, received, held = pl.pallas_call(
        kernel,
        out_shape=(
            pltpu.VMEM((PER // 4, 4, MLOC, BEAMS), BF),
            pltpu.VMEM((2, 4, PEERS, LOCAL, 16, 128), BF),
            pltpu.VMEM((PER // 4, 4, 2 * LOCAL * PEERS, BEAMS), BF),
        ),
        in_specs=[pl.BlockSpec(memory_space=pltpu.SMEM), pl.BlockSpec(memory_space=pltpu.VMEM), anywhere, anywhere, anywhere],
        out_specs=(whole, whole, whole),
        scratch_shapes=[
            pltpu.VMEM((LOCAL, 2, ROWS, 128), BF),
            pltpu.VMEM((LOCAL, 2, ROWS, 128), F32),
            pltpu.VMEM((TAPS, 2, 8, 128), F32),
            pltpu.VMEM((16 * FS, 128), F32),
            pltpu.VMEM((4, 256, CH // 2), BF),
            pltpu.VMEM((4, CH // 2, CH // 2), BF),
            pltpu.VMEM((2, 4, PEERS, LOCAL, 16, 128), BF),
            pltpu.VMEM((16 * XS, 128), F32),
            pltpu.SemaphoreType.DMA((LOCAL,)),
            pltpu.SemaphoreType.DMA,
            pltpu.SemaphoreType.DMA,
            pltpu.SemaphoreType.DMA((2,)),
            pltpu.SemaphoreType.DMA((2,)),
            pltpu.SemaphoreType.DMA((5,)),
            pltpu.SemaphoreType.DMA((5,)),
        ],
        compiler_params=pltpu.CompilerParams(collective_id=0, has_side_effects=True, vmem_limit_bytes=26 << 20),
        name="channelize_beams",
    )(delays, fir_coeffs, rows, weights, jnp.asarray(twiddle_table()))
    power = pl.pallas_call(
        tail_kernel,
        out_shape=jax.ShapeDtypeStruct((PER // 4, 4, MLOC, BEAMS), BF),
        in_specs=[whole, whole, whole],
        out_specs=anywhere,
        scratch_shapes=[
            pltpu.VMEM((16 * XS, 128), F32),
            pltpu.VMEM((PER // 4, HALF, BEAMS), BF),
            pltpu.SemaphoreType.DMA((4,)),
            pltpu.SemaphoreType.DMA,
        ],
        compiler_params=pltpu.CompilerParams(vmem_limit_bytes=8 << 20),
        name="tail_beams",
    )(*[pltpu.with_memory_space_constraint(v, pltpu.VMEM) for v in (done, received, held)])
    return power.reshape(PER, MLOC, BEAMS)


def solution(mesh):
    placed = (P("stn", None, None, "tm"), P("stn"), P(), P("stn", None, None, None))
    return jax.shard_map(
        per_device, mesh=mesh, in_specs=placed, out_specs=P("stn", "tm", None), check_vma=False
    )
```

```python
import math

import jax
import jax.numpy as jnp
import ml_dtypes
import numpy as np
from jax import lax
from jax.experimental import pallas as pl
from jax.experimental.pallas import tpu as pltpu
from jax.sharding import PartitionSpec as P

MESH = pl.DeviceIdType.MESH
BF, F32 = jnp.bfloat16, jnp.float32
CH, TAPS, BEAMS, DMAX = 1024, 16, 1024, 4096
PEERS = 32
LOCAL = 4
PER = CH // PEERS
MLOC = 128
HALF = MLOC // 2
FIRST = 16
LEAD = TAPS - 1
FRAMES = LEAD + MLOC + DMAX // CH
ROWS = FRAMES * 16 + 16
LEAD_ROWS, OWN_ROWS, TRAIL_ROWS = LEAD * 16, MLOC * 16, DMAX // CH * 16
FS = 136
XS = 136


def twiddle_table():
    n = np.arange(CH // 4)
    out = np.zeros((4, PEERS, PER // 4, 2, 2, CH // 4), np.float64)
    for r in range(4):
        k = PER * np.arange(PEERS)[:, None] + 4 * np.arange(PER // 4)[None, :] + r
        angle = 2 * np.pi * ((k[:, :, None] * n) % CH) / CH
        cosine, sine = np.cos(angle) / math.sqrt(CH), np.sin(angle) / math.sqrt(CH)
        out[r, :, :, 0, 0], out[r, :, :, 0, 1] = cosine, sine
        out[r, :, :, 1, 0], out[r, :, :, 1, 1] = -sine, cosine
    return out.reshape(4, CH // 2, CH // 2).astype(ml_dtypes.bfloat16)


def interleave(received, X):
    def body(g, carry):
        for s in range(LOCAL):
            X[pl.ds(g * LOCAL + s, 16, stride=XS), :] = received[g, s].astype(F32)
        return carry

    lax.fori_loop(0, PEERS, body, 0, unroll=4)


def beam(X, j, weights):
    rows = [pl.ds(pl.multiple_of((2 * j + c) * XS, 8), 128) for c in range(2)]
    re, im = [X[v, :].astype(BF).T for v in rows]
    lhs = jnp.concatenate([jnp.concatenate([re, -im], 1), jnp.concatenate([im, re], 1)], 0)
    y = jnp.dot(lhs, weights, preferred_element_type=F32)
    y = y * y
    power = (y[:HALF] + y[HALF : 2 * HALF]) + (y[2 * HALF : 3 * HALF] + y[3 * HALF :])
    return power.astype(BF)


def tail_kernel(done, R, W, out, X, O, done_sem, tail_sem):
    last = 3
    copies = [pltpu.make_async_copy(done.at[:, r], out.at[:, r], done_sem.at[r]) for r in range(last)]
    half = pl.ds(FIRST, HALF)
    copies.append(pltpu.make_async_copy(done.at[:, last, half], out.at[:, last, half], done_sem.at[last]))
    for copy in copies:
        copy.start()
    interleave(R.at[1, last], X)

    def body(j, carry):
        O[j] = beam(X, j, W[j, last])
        head = MLOC - FIRST - HALF
        pltpu.make_async_copy(O.at[j, pl.ds(0, head)], out.at[j, last, pl.ds(FIRST + HALF, head)], tail_sem).start()
        pltpu.make_async_copy(O.at[j, pl.ds(head, FIRST)], out.at[j, last, pl.ds(0, FIRST)], tail_sem).start()
        return carry

    lax.fori_loop(0, PER // 4, body, 0, unroll=2)
    for copy in copies:
        copy.wait()
    pltpu.make_async_copy(O, O, tail_sem).wait()


def kernel(delays, coef, base, weights, table, out, R, W, raw, E, C, Fq, F, T, S, X,
           base_sem, table_sem, weight_sem, halo_send, halo_recv, send_sem, recv_sem):
    t, me = lax.axis_index("tm"), lax.axis_index("stn")
    mz, my, mx = me // 16, (me // 4) % 4, me % 4

    planes = [lax.rem(mz + i, 2) * 16 for i in range(2)]
    lines = [lax.rem(my + i, 4) * 4 for i in range(4)]
    columns = [lax.rem(mx + i, 4) for i in range(4)]

    def peer(i):
        q = (i * 13) % PEERS
        return planes[q // 16] + lines[(q // 4) % 4] + columns[q % 4]

    def at(stn):
        return {"tm": t, "stn": stn}

    def base_copy(s):
        return pltpu.make_async_copy(base.at[s], raw.at[s, :, pl.ds(LEAD_ROWS, OWN_ROWS)], base_sem.at[s])

    base_copy(0).start()

    barrier = pltpu.get_barrier_semaphore()

    def greet(i, carry):
        pl.semaphore_signal(barrier, inc=1, device_id=at(peer(i)), device_id_type=MESH)
        return carry

    for i in range(1, PEERS):
        greet(i, 0)

    @pl.when(t > 0)
    def _():
        pl.semaphore_signal(barrier, inc=1, device_id={"tm": t - 1, "stn": me}, device_id_type=MESH)

    @pl.when(t < 3)
    def _():
        pl.semaphore_signal(barrier, inc=1, device_id={"tm": t + 1, "stn": me}, device_id_type=MESH)

    for s in range(1, LOCAL):
        base_copy(s).start()
    table_copy = pltpu.make_async_copy(table, T, table_sem)
    table_copy.start()
    weight_copy = pltpu.make_async_copy(weights, W, weight_sem)

    ahead = raw.at[:, :, pl.ds(0, LEAD_ROWS)], raw.at[:, :, pl.ds(LEAD_ROWS + OWN_ROWS, TRAIL_ROWS)]

    def send_halo(which):
        to = {"tm": t + 1 - 2 * which, "stn": me}

        parts = 5 if which == 0 else 1
        size = (LEAD_ROWS if which == 0 else TRAIL_ROWS) // parts
        start = OWN_ROWS - LEAD_ROWS if which == 0 else 0
        place = 0 if which == 0 else LEAD_ROWS + OWN_ROWS

        def body(i, carry):
            s, p = (i // 2) % LOCAL, i % 2
            at_row = pl.multiple_of(size * (i // (2 * LOCAL)), 16)
            pltpu.make_async_remote_copy(
                base.at[s, p, pl.ds(start + at_row, size)], raw.at[s, p, pl.ds(place + at_row, size)],
                halo_send.at[which], halo_recv.at[which], device_id=to, device_id_type=MESH).start()
            return carry

        lax.fori_loop(0, 2 * LOCAL * parts, body, 0)

    def halo_wait(sems, which):
        pltpu.make_async_copy(ahead[which], ahead[which], sems.at[which]).wait()

    def rotate(s, shift, first, count):
        j = lax.broadcasted_iota(jnp.int32, (128, 128), 0)
        lane = lax.broadcasted_iota(jnp.int32, (128, 128), 1)
        rotation = jnp.where((j == lane + shift) | (j == lane + shift - 128), 1.0, 0.0).astype(BF)

        def body(p, carry):
            rows = pl.ds(first * 16, count * 16)
            E[s, p, rows, :] = jnp.dot(raw[s, p, rows, :], rotation, preferred_element_type=F32)
            return carry

        lax.fori_loop(0, 2, body, 0)

    def fir(s, h, tiles, shift):
        keep = lax.broadcasted_iota(jnp.int32, (8, 128), 1) < 128 - shift

        def body(it, carry):
            i, p, half = it // 4, (it // 2) % 2, it % 2
            first = (FIRST + HALF * h + 16 * i) % MLOC
            d = []
            for f in range(31):
                row = (first + f) * 16 + half * 8 + 2 * tiles
                d.append(jnp.where(keep, E[s, p, pl.ds(row, 8), :], E[s, p, pl.ds(row + 2, 8), :]))
            for m in range(16):
                total = C[0, half] * d[m]
                for k in range(1, TAPS):
                    total = total + C[k, half] * d[m + k]
                Fq[pl.ds(half * 8 * FS + p * HALF + i * 16 + m, 8, stride=FS), :] = total
            return carry

        lax.fori_loop(0, 16, body, 0)

    def butterfly(place):
        def body(block, carry):
            rows = pl.multiple_of(block * 16, 16)
            for low in range(2):
                x = [[Fq[pl.ds(rows + ((2 * q + low) * 2 + c) * FS, 16), :] for q in range(4)] for c in range(2)]
                t0, t1 = [v[0] + v[2] for v in x], [v[0] - v[2] for v in x]
                t2, t3 = [v[1] + v[3] for v in x], [v[1] - v[3] for v in x]
                y = [
                    [t0[0] + t2[0], t0[1] + t2[1]],
                    [t1[0] + t3[1], t1[1] - t3[0]],
                    [t0[0] - t2[0], t0[1] - t2[1]],
                    [t1[0] - t3[1], t1[1] + t3[0]],
                ]
                for r in range(4):
                    for c in range(2):
                        lanes = c * 256 + low * 128
                        F[r, pl.ds(place * 128 + rows, 16), lanes : lanes + 128] = y[r][c].astype(BF)
            return carry

        lax.fori_loop(0, 8, body, 0)

    def transform(h, first, count):
        def body(r, carry):
            rows = F[r] if count == 2 else F[r, :128]
            spectra = lax.dot_general(T[r], rows, (((1,), (1,)), ((), ())), preferred_element_type=F32).astype(BF)
            for i in range(count):
                S[h, r, :, first + i] = spectra[:, 128 * i : 128 * i + 128].reshape(PEERS, 16, 128)
            return carry

        lax.fori_loop(0, 4, body, 0)

    def filtered(h, s, place):
        delay = delays[s]
        fir(s, h, delay // 128, delay % 128)
        butterfly(place)

    def send_first(s, count):
        def body(i, carry):
            d = peer(i)
            one = pl.ds(s, count)
            pltpu.make_async_remote_copy(
                S.at[0, :, d, one], R.at[0, :, me, one], send_sem.at[0], recv_sem.at[0],
                device_id=at(d), device_id_type=MESH).start()
            return carry

        for i in range(1, PEERS):
            body(i, 0)

    def send_second(r):
        def body(i, carry):
            d = peer(i)
            pltpu.make_async_remote_copy(
                S.at[1, r, d], R.at[1, r, me], send_sem.at[1 + r], recv_sem.at[1 + r],
                device_id=at(d), device_id_type=MESH).start()
            return carry

        for i in range(1, PEERS):
            body(i, 0)
        pltpu.make_async_copy(S.at[1, r, me], R.at[1, r, me], recv_sem.at[1 + r]).start()

    def beams(h, r):
        interleave(R.at[h, r], X)

        def body(j, carry):
            power = beam(X, j, W[j, r])
            if h == 0:
                out[j, r, FIRST : FIRST + HALF, :] = power
            else:
                out[j, r, FIRST + HALF :, :] = power[: MLOC - FIRST - HALF]
                out[j, r, :FIRST, :] = power[MLOC - FIRST - HALF :]
            return carry

        lax.fori_loop(0, PER // 4, body, 0, unroll=4)

    pl.semaphore_wait(barrier, PEERS - 1 + (t + 2) // 3 + (5 - t) // 3)
    pl.when(t < 3)(lambda: send_halo(0))
    pl.when(t > 0)(lambda: send_halo(1))

    for k in range(TAPS):
        for j in range(8):
            pair = jnp.broadcast_to(coef[k : k + 1, 128 * j : 128 * j + 128], (2, 128))
            C[k, j // 4, 2 * (j % 4) : 2 * (j % 4) + 2, :] = pair
    raw[:, :, FRAMES * 16 :, :] = jnp.zeros((LOCAL, 2, 16, 128), BF)

    @pl.when(t == 0)
    def _():
        raw[:, :, :LEAD_ROWS, :] = jnp.zeros((LOCAL, 2, LEAD_ROWS, 128), BF)

    @pl.when(t == 3)
    def _():
        raw[:, :, LEAD_ROWS + OWN_ROWS : FRAMES * 16, :] = jnp.zeros((LOCAL, 2, TRAIL_ROWS, 128), BF)

    def first_rows(s):
        base_copy(s).wait()
        rotate(s, delays[s] % 128, 16, 84)

    first_rows(0)

    def first(s, carry):
        pl.when(s > 0)(lambda: first_rows(s))
        filtered(0, s, 0)
        pl.when(s == 0)(table_copy.wait)
        transform(0, s, 1)
        send_first(s, 1)
        pl.when(s == 0)(weight_copy.start)
        return carry

    lax.fori_loop(0, 2, first, 0)

    def both(i, carry):
        first_rows(2 + i)
        filtered(0, 2 + i, i)
        return carry

    lax.fori_loop(0, 2, both, 0)
    transform(0, 2, 2)
    send_first(2, 2)
    pltpu.make_async_copy(S.at[0, :, me], R.at[0, :, me], recv_sem.at[0]).start()
    pl.when(t > 0)(lambda: halo_wait(halo_recv, 0))
    pl.when(t < 3)(lambda: halo_wait(halo_recv, 1))

    def second(pair, carry):
        def body(i, carry):
            s = 2 * pair + i
            rotate(s, delays[s] % 128, 0, 16)
            rotate(s, delays[s] % 128, 100, 48)
            filtered(1, s, i)
            return carry

        lax.fori_loop(0, 2, body, 0)
        transform(1, 2 * pair, 2)
        return carry

    lax.fori_loop(0, 2, second, 0)
    send_second(0)
    weight_copy.wait()
    pltpu.make_async_copy(R.at[0], R.at[0], recv_sem.at[0]).wait()

    def finish_first(r, carry):
        pl.when(r < 3)(lambda: send_second(r + 1))
        beams(0, r)
        return carry

    lax.fori_loop(0, 4, finish_first, 0)

    def finish_second(r, carry):
        pltpu.make_async_copy(R.at[1, r], R.at[1, r], recv_sem.at[1 + r]).wait()
        pl.when(r < 3)(lambda: beams(1, r))
        return carry

    lax.fori_loop(0, 4, finish_second, 0)

    sent = pl.ds(0, PEERS - 1)
    pltpu.make_async_copy(S.at[0, :, sent], S.at[0, :, sent], send_sem.at[0]).wait()

    def sent_second(r, carry):
        pltpu.make_async_copy(S.at[1, r, sent], S.at[1, r, sent], send_sem.at[1 + r]).wait()
        return carry

    lax.fori_loop(0, 4, sent_second, 0)

    pl.when(t < 3)(lambda: halo_wait(halo_send, 0))
    pl.when(t > 0)(lambda: halo_wait(halo_send, 1))


def per_device(baseband, delays, fir_coeffs, beam_weights):
    rows = baseband.reshape(LOCAL, 2, 2, OWN_ROWS // 2, 128).transpose(0, 1, 3, 2, 4).reshape(LOCAL, 2, OWN_ROWS, 128)
    weights = beam_weights.reshape(PER // 4, 4, 2 * LOCAL * PEERS, BEAMS)
    anywhere = pl.BlockSpec(memory_space=pl.ANY)
    whole = pl.BlockSpec(memory_space=pltpu.VMEM)
    done, received, held = pl.pallas_call(
        kernel,
        out_shape=(
            pltpu.VMEM((PER // 4, 4, MLOC, BEAMS), BF),
            pltpu.VMEM((2, 4, PEERS, LOCAL, 16, 128), BF),
            pltpu.VMEM((PER // 4, 4, 2 * LOCAL * PEERS, BEAMS), BF),
        ),
        in_specs=[pl.BlockSpec(memory_space=pltpu.SMEM), pl.BlockSpec(memory_space=pltpu.VMEM), anywhere, anywhere, anywhere],
        out_specs=(whole, whole, whole),
        scratch_shapes=[
            pltpu.VMEM((LOCAL, 2, ROWS, 128), BF),
            pltpu.VMEM((LOCAL, 2, ROWS, 128), F32),
            pltpu.VMEM((TAPS, 2, 8, 128), F32),
            pltpu.VMEM((16 * FS, 128), F32),
            pltpu.VMEM((4, 256, CH // 2), BF),
            pltpu.VMEM((4, CH // 2, CH // 2), BF),
            pltpu.VMEM((2, 4, PEERS, LOCAL, 16, 128), BF),
            pltpu.VMEM((16 * XS, 128), F32),
            pltpu.SemaphoreType.DMA((LOCAL,)),
            pltpu.SemaphoreType.DMA,
            pltpu.SemaphoreType.DMA,
            pltpu.SemaphoreType.DMA((2,)),
            pltpu.SemaphoreType.DMA((2,)),
            pltpu.SemaphoreType.DMA((5,)),
            pltpu.SemaphoreType.DMA((5,)),
        ],
        compiler_params=pltpu.CompilerParams(collective_id=0, has_side_effects=True, vmem_limit_bytes=26 << 20),
        name="channelize_beams",
    )(delays, fir_coeffs, rows, weights, jnp.asarray(twiddle_table()))
    power = pl.pallas_call(
        tail_kernel,
        out_shape=jax.ShapeDtypeStruct((PER // 4, 4, MLOC, BEAMS), BF),
        in_specs=[whole, whole, whole],
        out_specs=anywhere,
        scratch_shapes=[
            pltpu.VMEM((16 * XS, 128), F32),
            pltpu.VMEM((PER // 4, HALF, BEAMS), BF),
            pltpu.SemaphoreType.DMA((4,)),
            pltpu.SemaphoreType.DMA,
        ],
        compiler_params=pltpu.CompilerParams(vmem_limit_bytes=8 << 20),
        name="tail_beams",
    )(*[pltpu.with_memory_space_constraint(v, pltpu.VMEM) for v in (done, received, held)])
    return power.reshape(PER, MLOC, BEAMS)


def solution(mesh):
    placed = (P("stn", None, None, "tm"), P("stn"), P(), P("stn", None, None, None))
    return jax.shard_map(
        per_device, mesh=mesh, in_specs=placed, out_specs=P("stn", "tm", None), check_vma=False
    )
```
